256 devices in a mesh: dp: 8 (over x, core), expert: 32 (over y, z).
Axes of the slice: x: 4, y: 4, z: 8, core: 2. Of those that a mesh axis runs over, the one named last changes fastest.
Arguments:
- tokens: bfloat16 [32768, 7168], P(('dp', 'expert')), may hold values from -6 to 6
- out_grad: bfloat16 [32768, 7168], P(('dp', 'expert')), may hold values from -6 to 6
- expert_ids: int32 [32768, 8], P(('dp', 'expert')), may hold values from 0 to 255, as said below
- route_probs: float32 [32768, 8], P(('dp', 'expert')), may hold values from 0.1 to 1
- hosted: int32 [8], replicated, may hold values from 0 to 255, as said below
- gate_weight: bfloat16 [7168, 16384], P('dp', 'expert'), may hold values from -0.0625 to 0.0625
- up_weight: bfloat16 [7168, 16384], P('dp', 'expert'), may hold values from -0.0625 to 0.0625
- down_weight: bfloat16 [16384, 7168], P('expert', 'dp'), may hold values from -0.125 to 0.125
Outputs:
- mixed: bfloat16 [32768, 7168], P(('dp', 'expert'))
- input_grad: bfloat16 [32768, 7168], P(('dp', 'expert'))
- prob_grad: float32 [32768, 8], P(('dp', 'expert'))
- gate_grad: bfloat16 [7168, 16384], P('dp', 'expert')
- up_grad: bfloat16 [7168, 16384], P('dp', 'expert')
- down_grad: bfloat16 [16384, 7168], P('expert', 'dp')
The draws below stay inside these ranges and needn't reach their ends.
Inputs may be any that keep to these rules, and one draw needn't show every extreme that they name: `expert_ids`: each row names 8 different experts; among the rows of one device, every hosted expert is named at most 4 times, and one hosted expert exactly 4 times on every device. `hosted`: 8 different experts, one of them expert 256 - 1.
All inputs are finite; a program needn't handle non-finite values.
Results may differ from the reference program's by a relative error of at most 0.0065.
Values may be sent and summed in bfloat16 or wider, within the bound.
A program may use at most 128 MiB of HBM per device.

```python
import jax
import jax.numpy as jnp
from jax import lax

D = 7168
HID = 2048
ROUTED = 256
TOP = 8
TOK_DEV = 128
WIN = 8
CAP = 4
TOKENS = 32768
N_EXPERT = 32


def route_plan(key):
    base = jax.random.permutation(jax.random.fold_in(key, 101), ROUTED).astype(jnp.int32)
    where_top = jnp.argmax(base == ROUTED - 1).astype(jnp.int32)
    top_slot = jax.random.randint(jax.random.fold_in(key, 109), (), 0, WIN).astype(jnp.int32)
    slot_value = base[top_slot]
    places = jnp.arange(ROUTED, dtype=jnp.int32)
    shuffled = jnp.where(places == top_slot, ROUTED - 1, jnp.where(places == where_top, slot_value, base)).astype(jnp.int32)
    hosted = shuffled[:WIN]
    blocks = TOKENS // TOK_DEV
    hot_index = jax.random.randint(jax.random.fold_in(key, 102), (), 0, WIN).astype(jnp.int32)
    shift_by = jax.random.randint(jax.random.fold_in(key, 103), (blocks, 1), 0, TOK_DEV).astype(jnp.int32)
    position = (jnp.arange(TOK_DEV, dtype=jnp.int32)[None, :] + shift_by) % TOK_DEV
    offset = jax.random.randint(jax.random.fold_in(key, 104), (blocks, TOK_DEV, 1), 0, ROUTED - WIN).astype(jnp.int32)
    spread = (offset + jnp.arange(TOP, dtype=jnp.int32)[None, None, :]) % (ROUTED - WIN)
    others = shuffled[WIN + spread]
    first_slot = jax.random.randint(jax.random.fold_in(key, 105), (blocks, TOK_DEV), 0, TOP).astype(jnp.int32)
    second = (first_slot + 1 + jax.random.randint(jax.random.fold_in(key, 106), (blocks, TOK_DEV), 0, TOP - 1).astype(jnp.int32)) % TOP
    coin_one = jax.random.randint(jax.random.fold_in(key, 107), (blocks, TOK_DEV), 0, 2).astype(jnp.int32)
    coin_two = jax.random.randint(jax.random.fold_in(key, 108), (blocks, TOK_DEV), 0, 2).astype(jnp.int32)
    in_hot = position < CAP
    range_index = (position - CAP) // (CAP - 1)
    in_range = (position >= CAP) & (range_index < WIN - 1)
    range_expert = (hot_index + 1 + range_index) % WIN
    extra_expert = (hot_index + 1 + position) % WIN
    slot_index = jnp.arange(TOP, dtype=jnp.int32)[None, None, :]
    first_other = jnp.take_along_axis(others, first_slot[..., None], axis=2)[..., 0]
    second_other = jnp.take_along_axis(others, second[..., None], axis=2)[..., 0]
    first_id = jnp.where(in_hot, hosted[hot_index], jnp.where(in_range & (coin_one == 1), hosted[range_expert], first_other))
    second_id = jnp.where(in_hot & (coin_two == 1), hosted[extra_expert], second_other)
    chosen_ids = jnp.where(slot_index == first_slot[..., None], first_id[..., None], others)
    chosen_ids = jnp.where(slot_index == second[..., None], second_id[..., None], chosen_ids)
    return (chosen_ids.reshape(TOKENS, TOP).astype(jnp.int32), hosted)


def draw_expert_ids(key, part):
    chosen_ids, hosted = route_plan(key)
    return chosen_ids


def draw_hosted(key, part):
    chosen_ids, hosted = route_plan(key)
    return hosted


def block_scale(stream_key, shape, shards, smallest, largest):
    level, own = 1.0, jax.random.fold_in(stream_key, 6)
    for dim, blocks in shards:
        steps = jnp.exp(jax.random.uniform(jax.random.fold_in(own, dim), (blocks,), jnp.float32, smallest / len(shards), largest / len(shards)))
        level = level * jnp.repeat(steps, shape[dim] // blocks).reshape([-1 if axis == dim else 1 for axis in range(len(shape))])
    return level


def normal_values(rng, shape, scale, reach, split=(), held_as=jnp.bfloat16):
    result = scale * jax.random.normal(rng, shape, jnp.float32)
    if split:
        result = result * block_scale(rng, shape, split, -0.22, 0.18)
    return jnp.clip(result, -reach, reach).astype(held_as)


def setup_inputs(seed: int = 0) -> dict:
    keys = jax.random.split(jax.random.key(seed), 9)
    return {
        "tokens": normal_values(keys[0], (TOKENS, D), 1.0, 6.0, ((0, 256),)),
        "out_grad": normal_values(keys[1], (TOKENS, D), 1.0, 6.0, ((0, 256),)),
        "expert_ids": draw_expert_ids(jax.random.fold_in(keys[8], 71), 0),
        "route_probs": jnp.clip(0.1 + 0.9 * jax.random.uniform(keys[3], (TOKENS, TOP), jnp.float32) ** block_scale(keys[3], (TOKENS, TOP), ((0, 256),), -0.2, 0.2), 0.1, 1.0),
        "hosted": draw_hosted(jax.random.fold_in(keys[8], 71), 0),
        "gate_weight": normal_values(keys[5], (D, WIN * HID), D ** -0.5, 0.0625, ((0, 8), (1, 32))),
        "up_weight": normal_values(keys[6], (D, WIN * HID), D ** -0.5, 0.0625, ((0, 8), (1, 32))),
        "down_weight": normal_values(keys[7], (WIN * HID, D), HID ** -0.5, 0.125, ((0, 32), (1, 8))),
    }


def slot_picks(block_ids, hosted):
    tok_count = block_ids.shape[0]
    matches = (block_ids.reshape(tok_count * TOP, 1) == hosted[None, :]).astype(jnp.int32)
    rank_in = jnp.cumsum(matches, axis=0) - matches
    expert_pos = jnp.arange(WIN, dtype=jnp.int32)[None, :]
    target = jnp.sum(matches * (expert_pos * CAP + rank_in), axis=1) + (1 - jnp.sum(matches, axis=1)) * (WIN * CAP)
    picked = (target[:, None] == jnp.arange(WIN * CAP, dtype=jnp.int32)[None, :]).astype(jnp.int32)
    return picked.reshape(tok_count, TOP, WIN * CAP)


def activate(gate_pre, up_pre, back):
    sigmoid_g = jax.nn.sigmoid(gate_pre)
    silu_gate = gate_pre * sigmoid_g
    hidden = (silu_gate * up_pre).astype(jnp.bfloat16)
    grad_gate = (back * up_pre * sigmoid_g * (1.0 + gate_pre * (1.0 - sigmoid_g))).astype(jnp.bfloat16)
    grad_up = (back * silu_gate).astype(jnp.bfloat16)
    return hidden, grad_gate, grad_up


def reference(tokens, out_grad, expert_ids, route_probs, hosted, gate_weight, up_weight, down_weight):
    group_size = N_EXPERT // WIN
    blocks = TOKENS // TOK_DEV
    slot_count = WIN * CAP
    picked = jax.vmap(slot_picks, in_axes=(0, None))(expert_ids.reshape(blocks, TOK_DEV, TOP), hosted)
    chosen = jnp.sum(picked, axis=2)
    prob_table = jnp.sum(picked.astype(jnp.float32) * route_probs.reshape(blocks, TOK_DEV, TOP)[..., None], axis=2)
    position = jnp.sum(chosen * jnp.arange(TOK_DEV, dtype=jnp.int32)[None, :, None], axis=1).astype(jnp.int32)
    live = jnp.sum(chosen, axis=1)
    slot_prob = jnp.sum(prob_table, axis=1)
    tok_rows = jnp.take_along_axis(tokens.reshape(blocks, TOK_DEV, D), position[..., None], axis=1)
    tok_rows = jnp.where(live[..., None] > 0, tok_rows, jnp.zeros_like(tok_rows))
    grad_rows = jnp.take_along_axis(out_grad.reshape(blocks, TOK_DEV, D), position[..., None], axis=1)
    scaled = (slot_prob[..., None] * grad_rows.astype(jnp.float32)).astype(jnp.bfloat16)

    def by_expert(rows):
        return rows.reshape(blocks, WIN, CAP, D).transpose(1, 0, 2, 3).reshape(WIN, blocks * CAP, D)

    gate_w = gate_weight.reshape(D, WIN, HID).transpose(1, 0, 2)
    up_w = up_weight.reshape(D, WIN, HID).transpose(1, 0, 2)
    down_w = down_weight.reshape(WIN, HID, D)
    block_len = HID // group_size

    def one_expert(operands):
        tok_in, grad_in, gate_m, up_m, down_m = operands
        gate_pre = jnp.dot(tok_in, gate_m, preferred_element_type=jnp.float32)
        up_pre = jnp.dot(tok_in, up_m, preferred_element_type=jnp.float32)
        back = jnp.dot(grad_in, down_m.T, preferred_element_type=jnp.float32)
        hidden, grad_gate, grad_up = activate(gate_pre, up_pre, back)
        expert_out = jnp.zeros((tok_in.shape[0], D), jnp.float32)
        token_back = jnp.zeros((tok_in.shape[0], D), jnp.float32)
        for index in range(group_size):
            low = index * block_len
            high = low + block_len
            piece_out = jnp.dot(hidden[:, low:high], down_m[low:high], preferred_element_type=jnp.float32).astype(jnp.bfloat16)
            expert_out = expert_out + lax.optimization_barrier(piece_out).astype(jnp.float32)
            piece_back = jnp.dot(grad_gate[:, low:high], gate_m[:, low:high].T, preferred_element_type=jnp.float32)
            piece_back = piece_back + jnp.dot(grad_up[:, low:high], up_m[:, low:high].T, preferred_element_type=jnp.float32)
            token_back = token_back + lax.optimization_barrier(piece_back.astype(jnp.bfloat16)).astype(jnp.float32)
        gate_dw = jnp.dot(tok_in.T, grad_gate, preferred_element_type=jnp.float32).astype(jnp.bfloat16)
        up_dw = jnp.dot(tok_in.T, grad_up, preferred_element_type=jnp.float32).astype(jnp.bfloat16)
        down_dw = jnp.dot(hidden.T, grad_in, preferred_element_type=jnp.float32).astype(jnp.bfloat16)
        return expert_out, token_back, gate_dw, up_dw, down_dw

    results = lax.map(one_expert, (by_expert(tok_rows), by_expert(scaled), gate_w, up_w, down_w))

    def by_block(rows):
        return rows.reshape(WIN, blocks, CAP, D).transpose(1, 0, 2, 3).reshape(blocks, slot_count, D)

    expert_outs = by_block(results[0])
    token_backs = by_block(results[1])
    highest = lax.Precision.HIGHEST
    mixed = jnp.einsum('bts,bsd->btd', prob_table, expert_outs, precision=highest)
    input_grad = jnp.einsum('bts,bsd->btd', chosen.astype(jnp.float32), token_backs, precision=highest)
    scores = jnp.einsum('btd,bsd->bts', out_grad.reshape(blocks, TOK_DEV, D).astype(jnp.float32), expert_outs, precision=highest)
    prob_grad = jnp.sum(picked.astype(jnp.float32) * scores[:, :, None, :], axis=3)
    gate_grad = results[2].transpose(1, 0, 2).reshape(D, WIN * HID)
    up_grad = results[3].transpose(1, 0, 2).reshape(D, WIN * HID)
    down_grad = results[4].reshape(WIN * HID, D)
    return (mixed.reshape(TOKENS, D).astype(jnp.bfloat16), input_grad.reshape(TOKENS, D).astype(jnp.bfloat16),
            prob_grad.reshape(TOKENS, TOP), gate_grad, up_grad, down_grad)
```

```python
import functools

import jax
import jax.numpy as jnp
from jax import lax
from jax.experimental import pallas as pl
from jax.experimental.pallas import tpu as pltpu
from jax.sharding import PartitionSpec as P

CAP = 4
BF = jnp.bfloat16
F32 = jnp.float32
MESH = pl.DeviceIdType.MESH
NT = (((1,), (1,)), ((), ()))
TN = (((0,), (0,)), ((), ()))
R, L = 0, 1


def kernel(
    width,
    ids_ref, probs_ref, hosted_ref, tokens_hbm, ograd_hbm, wg_hbm, wu_hbm, wd_hbm,
    mixed_hbm, igrad_hbm, pgrad_ref, ggrad_hbm, ugrad_hbm, dgrad_hbm,
    tokens, ograd, wg, wu, wd, mixed, igrad, ggrad, ugrad, dgrad,
    xsend, xbuf, ysend, zsrc, tokin,
    part, rs, xr1, fin, own, acts,
    outp, rbuf, zout, yback, xback, eo, perm, permt,
    insem, outsem, xs_s, xs_r, ys_s, ys_r, zs_s, zs_r,
    cx_s, cx_r, rx_s, rx_r, ag_s, ag_r,
    zb_s, zb_r, yb_s, yb_r, xb_s, xb_r,
):
    me_dp = lax.axis_index("dp")
    me_e = lax.axis_index("expert")
    x, c = lax.div(me_dp, 2), lax.rem(me_dp, 2)
    y, z = lax.div(me_e, 8), lax.rem(me_e, 8)
    myhalf = lax.div(z, 4)

    def dev(x_, c_, y_, z_):
        return (x_ * 2 + c_, y_ * 8 + z_)

    def rcopy(src, dst, ssem, rsem, where):
        return pltpu.make_async_remote_copy(
            src_ref=src, dst_ref=dst, send_sem=ssem, recv_sem=rsem,
            device_id=where, device_id_type=MESH,
        )

    other_core = dev(x, 1 - c, y, z)
    xr_dev = dev(lax.rem(x + 1, 4), c, y, z)
    xl_dev = dev(lax.rem(x + 3, 4), c, y, z)
    zr_dev = dev(x, c, y, lax.rem(z + 1, 8))
    zl_dev = dev(x, c, y, lax.rem(z + 7, 8))

    def wait_in(dst, rsem):
        rcopy(dst, dst, rsem, rsem, other_core).wait_recv()

    loads = [
        pltpu.make_async_copy(a, b, insem.at[i])
        for i, (a, b) in enumerate(
            ((tokens_hbm, tokens), (ograd_hbm, ograd), (wg_hbm, wg), (wu_hbm, wu), (wd_hbm, wd))
        )
    ]
    for load in loads:
        load.start()

    barrier = pltpu.get_barrier_semaphore()
    partners = []
    for kx in range(4):
        for kc in range(2):
            if kx or kc:
                partners.append(dev(lax.rem(x + kx, 4), lax.rem(c + kc, 2), y, z))
    for k in range(1, 4):
        partners.append(dev(x, c, lax.rem(y + k, 4), z))
    partners += [zr_dev, zl_dev]
    for partner in partners:
        pl.semaphore_signal(barrier, inc=1, device_id=partner, device_id_type=MESH)

    ids = ids_ref[...]
    probs = probs_ref[...]
    hosted = hosted_ref[...]
    matched = jnp.zeros((128, 128), F32)
    prob_at = jnp.zeros((128, 128), F32)
    for k in range(8):
        hit = (ids[:, k : k + 1] == hosted).astype(F32)
        matched = matched + hit
        prob_at = prob_at + hit * probs[:, k : k + 1]
    row = lax.broadcasted_iota(jnp.int32, (128, 128), 0)
    lane = lax.broadcasted_iota(jnp.int32, (128, 128), 1)
    before = (lane < row).astype(BF)
    rank = jnp.dot(before, matched.astype(BF), preferred_element_type=F32)
    chosen = matched * (rank == (lane & 3).astype(F32)).astype(F32)
    table = prob_at * chosen
    chosen32 = jnp.where(lane < 32, chosen, 0.0)
    select = chosen32.T[:32].astype(BF)
    slot_prob = jnp.sum(table.T[:32], axis=1, keepdims=True)

    prow = lax.broadcasted_iota(jnp.int32, (256, 256), 0)
    plane = lax.broadcasted_iota(jnp.int32, (256, 256), 1)

    def moved(q):
        return ((q >> 2) & 7) * 32 + (q >> 6) * 8 + ((q >> 5) & 1) * 4 + (q & 3)

    perm[...] = (plane == moved(prow)).astype(BF)
    permt[...] = (prow == moved(plane)).astype(BF)

    pl.semaphore_wait(barrier, len(partners))

    def x_copy(arr, kx, kc, back):
        xd, cd = lax.rem(x + kx, 4), lax.rem(c + kc, 2)
        there = xd * 2 + cd
        k = kx * 2 + kc
        if back:
            return rcopy(xback.at[arr, there], eo.at[arr, me_dp], xb_s.at[arr, k], xb_r.at[arr, k], dev(xd, cd, y, z))
        return rcopy(xsend.at[arr, there], xbuf.at[arr, me_dp], xs_s.at[arr, k], xs_r.at[arr, k], dev(xd, cd, y, z))

    def x_wait(arr, back):
        for kx in range(4):
            for kc in range(2):
                if kx or kc:
                    k = kx * 2 + kc
                    origin = lax.rem(x + 4 - kx, 4) * 2 + lax.rem(c + kc, 2)
                    if back:
                        wait_in(eo.at[arr, origin], xb_r.at[arr, k])
                    else:
                        wait_in(xbuf.at[arr, origin], xs_r.at[arr, k])

    order = ((2, 0), (2, 1), (1, 0), (3, 0), (1, 1), (3, 1), (0, 1))

    def gather_rows(arr):
        def share(index):
            columns = pl.ds(pl.multiple_of(index * width, 128), width)
            source = tokens if arr == 0 else ograd
            rows = jnp.dot(select, source[:, columns], preferred_element_type=F32)
            if arr == 1:
                rows = slot_prob * rows
            return rows.astype(BF)

        for kx, kc in order:
            there = lax.rem(x + kx, 4) * 2 + lax.rem(c + kc, 2)
            xsend[arr, there] = share(there)
            x_copy(arr, kx, kc, False).start()
        xbuf[arr, me_dp] = share(me_dp)

    def y_copy(arr, k, back):
        yd = lax.rem(y + k, 4)
        if back:
            src = zout.at[arr, :, pl.ds(pl.multiple_of(yd * 32, 32), 32)]
            return rcopy(src, yback.at[arr, y], yb_s.at[arr, k], yb_r.at[arr, k], dev(x, c, yd, z))
        dst = zsrc.at[arr, :, pl.ds(pl.multiple_of(y * 32, 32), 32)]
        return rcopy(ysend.at[arr, yd], dst, ys_s.at[arr, k], ys_r.at[arr, k], dev(x, c, yd, z))

    def y_stage(arr):
        x_wait(arr, False)
        rows = jnp.dot(perm[...], xbuf[arr].reshape(256, width), preferred_element_type=F32).astype(BF)
        ysend[arr] = rows.reshape(4, 2, 32, width)
        for k in (2, 1, 3):
            y_copy(arr, k, False).start()
        mine = pl.ds(pl.multiple_of(y * 32, 32), 32)
        zsrc[arr, :, mine] = ysend[arr, y]

    def y_wait(arr):
        for k in (1, 3, 2):
            origin = lax.rem(y + 4 - k, 4)
            wait_in(zsrc.at[arr, :, pl.ds(pl.multiple_of(origin * 32, 32), 32)], ys_r.at[arr, k])

    sign = (1, -1)
    onward = (zr_dev, zl_dev)
    backward = (zl_dev, zr_dev)
    start = (lax.rem(z + 2, 8), lax.rem(13 - z, 8))

    def place(d, half):
        return lax.rem(start[d] + 4 * half, 8)

    def origin_z(d, s):
        return lax.rem(z + 8 - sign[d] * s, 8)

    def z_send(arr, d, half, s):
        p = place(d, half)
        src = origin_z(d, s)

        @pl.when((p >= s) & (p <= 4))
        def _():
            if s == 0:
                first = lax.div(7 - p, 7)
                slot = src + first * (8 + d - src)
                rcopy(zsrc.at[arr, half], tokin.at[arr, slot], zs_s.at[arr, d, half, s], zs_r.at[arr, d, half, s + 1], onward[d]).start()
            else:
                held = src
                if s == 1:
                    second = lax.div(lax.rem(8 - p, 8), 7)
                    held = src + second * (8 + d - src)
                rcopy(tokin.at[arr, held], tokin.at[arr, src], zs_s.at[arr, d, half, s], zs_r.at[arr, d, half, s + 1], onward[d]).start()

    def z_sent(arr):
        for d in (R, L):
            for half in (0, 1):
                for s in range(5):
                    p = place(d, half)

                    @pl.when((p >= s) & (p <= 4))
                    def _():
                        rcopy(zsrc.at[arr, half], tokin.at[arr, 0], zs_s.at[arr, d, half, s], zs_r.at[arr, d, half, s + 1], onward[d]).wait_send()

    def z_step(arr, s):
        for d in (R, L):
            for half in (0, 1):
                if s > 0:
                    p = place(d, half)

                    @pl.when((p >= s) & (p <= 5))
                    def _():
                        src = origin_z(d, s)
                        slot = src
                        if s == 1:
                            second = lax.div(lax.rem(8 - p, 8), 7)
                            slot = src + second * (8 + d - src)
                        wait_in(tokin.at[arr, slot], zs_r.at[arr, d, half, s])
                if s < 5:
                    z_send(arr, d, half, s)

    def z_begin(arr):
        y_wait(arr)
        z_step(arr, 0)
        tokin[arr, z] = zsrc[arr, myhalf]

    def forward(arr):
        def body(i, carry):
            rows = tokin[arr, pl.ds(2 * i, 2)].reshape(256, width)
            if arr == 0:
                part[0, i] = jnp.dot(rows, wg[...], preferred_element_type=F32).reshape(2, 128, 512)
                part[1, i] = jnp.dot(rows, wu[...], preferred_element_type=F32).reshape(2, 128, 512)
            else:
                part[2, i] = lax.dot_general(rows, wd[...], NT, preferred_element_type=F32).reshape(2, 128, 512)
            return carry

        lax.fori_loop(0, 4, body, 0)
        c_copy(arr).start()

    kinds = (pl.ds(0, 2), pl.ds(2, 1))

    def c_copy(g):
        return rcopy(part.at[kinds[g], :, 1 - c], rs.at[kinds[g]], cx_s.at[g], cx_r.at[g], other_core)

    low, high = pl.ds(0, 256), pl.ds(256, 256)
    ahead, behind, across = lax.rem(x + 1, 4), lax.rem(x + 3, 4), lax.rem(x + 2, 4)

    def rx_copies(g):
        ks = kinds[g]
        return (
            rcopy(rs.at[ks, across, :, low], xr1.at[R, ks], rx_s.at[g, 0], rx_r.at[g, 0], xr_dev),
            rcopy(rs.at[ks, across, :, high], xr1.at[L, ks], rx_s.at[g, 1], rx_r.at[g, 1], xl_dev),
            rcopy(rs.at[ks, ahead, :, high], fin.at[0, ks], rx_s.at[g, 2], rx_r.at[g, 2], xr_dev),
            rcopy(rs.at[ks, behind, :, low], fin.at[1, ks], rx_s.at[g, 3], rx_r.at[g, 3], xl_dev),
            rcopy(xr1.at[R, ks], fin.at[2, ks], rx_s.at[g, 4], rx_r.at[g, 4], xr_dev),
            rcopy(xr1.at[L, ks], fin.at[3, ks], rx_s.at[g, 5], rx_r.at[g, 5], xl_dev),
        )

    def rs_one(g):
        c_copy(g).wait_recv()
        copies = rx_copies(g)

        def add(chunk):
            for j in ((0, 1), (2,))[g]:
                rs[j, chunk] = part[j, chunk, c] + rs[j, chunk]

        add(across)
        copies[0].start()
        copies[1].start()
        add(ahead)
        copies[2].start()
        add(behind)
        copies[3].start()
        add(x)

    def rs_two(g):
        copies = rx_copies(g)
        copies[0].wait_recv()
        for j in ((0, 1), (2,))[g]:
            xr1[R, j] = xr1[R, j] + rs[j, ahead, :, low]
        copies[4].start()
        copies[1].wait_recv()
        for j in ((0, 1), (2,))[g]:
            xr1[L, j] = xr1[L, j] + rs[j, behind, :, high]
        copies[5].start()

    def rs_end(g):
        copies = rx_copies(g)
        for k in range(2, 6):
            copies[k].wait_recv()
        for j in ((0, 1), (2,))[g]:
            own[j, :, low] = rs[j, x, :, low] + fin[1, j] + fin[2, j]
            own[j, :, high] = rs[j, x, :, high] + fin[0, j] + fin[3, j]

    def activate(g):
        gate = own[0]
        up = own[1]
        sig = jax.nn.sigmoid(gate)
        silu = gate * sig
        if g == 0:
            acts[0, me_dp] = (silu * up).astype(BF)
        else:
            back = own[2]
            acts[1, me_dp] = (back * up * sig * (1.0 + gate * (1.0 - sig))).astype(BF)
            acts[2, me_dp] = (back * silu).astype(BF)

    held = (pl.ds(0, 1), pl.ds(1, 2))

    def ag_copy(g, k):
        ks = held[g]
        before_me, after_me, far = behind * 2 + c, ahead * 2 + c, across * 2 + c
        what, where = (
            (acts.at[ks, me_dp], xr_dev),
            (acts.at[ks, me_dp], xl_dev),
            (acts.at[ks, me_dp], other_core),
            (acts.at[ks, before_me, :, low], xr_dev),
            (acts.at[ks, after_me, :, high], xl_dev),
            (acts.at[ks, before_me], other_core),
            (acts.at[ks, after_me], other_core),
            (acts.at[ks, far], other_core),
        )[k]
        return rcopy(what, what, ag_s.at[g, k], ag_r.at[g, k], where)

    def ag_wait(g, k):
        ks = held[g]
        o = 1 - c
        dst = (
            acts.at[ks, behind * 2 + c],
            acts.at[ks, ahead * 2 + c],
            acts.at[ks, x * 2 + o],
            acts.at[ks, across * 2 + c, :, low],
            acts.at[ks, across * 2 + c, :, high],
            acts.at[ks, behind * 2 + o],
            acts.at[ks, ahead * 2 + o],
            acts.at[ks, across * 2 + o],
        )[k]
        wait_in(dst, ag_r.at[g, k])

    def ag_one(g):
        for k in range(3):
            ag_copy(g, k).start()

    def ag_two(g):
        ag_wait(g, 0)
        ag_copy(g, 3).start()
        ag_copy(g, 5).start()
        ag_wait(g, 1)
        ag_copy(g, 4).start()
        ag_copy(g, 6).start()

    def ag_three(g):
        ag_wait(g, 3)
        ag_wait(g, 4)
        ag_copy(g, 7).start()
        for k in (2, 5, 6, 7):
            ag_wait(g, k)

    def partial_out(arr):
        def body(i, carry):
            two = pl.ds(2 * i, 2)
            if arr == 0:
                piece = jnp.dot(acts[0, two].reshape(256, 512), wd[...], preferred_element_type=F32)
            else:
                piece = lax.dot_general(acts[1, two].reshape(256, 512), wg[...], NT, preferred_element_type=F32)
                piece = piece + lax.dot_general(acts[2, two].reshape(256, 512), wu[...], NT, preferred_element_type=F32)
            outp[arr, two] = piece.astype(BF).reshape(2, 128, width)
            return carry

        lax.fori_loop(0, 4, body, 0)

    def zb_copy(arr, d, half, s, whole):
        src = outp.at[arr, origin_z(d, s)] if whole else rbuf.at[arr, d, half, s]
        return rcopy(src, rbuf.at[arr, d, half, s - 1], zb_s.at[arr, d, half, s], zb_r.at[arr, d, half, s - 1], backward[d])

    def zb_begin(arr):
        for s in (5, 4, 3, 2, 1):
            for d in (R, L):
                for half in (0, 1):

                    @pl.when(place(d, half) == 5)
                    def _():
                        zb_copy(arr, d, half, s, True).start()

    def zb_step(arr, s):
        for d in (R, L):
            for half in (0, 1):
                p = place(d, half)

                @pl.when((p >= s) & (p <= 4))
                def _():
                    wait_in(rbuf.at[arr, d, half, s], zb_r.at[arr, d, half, s])
                    if s > 0:

                        @pl.when(p >= 2)
                        def _():
                            total = rbuf[arr, d, half, s].astype(F32) + outp[arr, origin_z(d, s)].astype(F32)
                            rbuf[arr, d, half, s] = total.astype(BF)

                        zb_copy(arr, d, half, s, False).start()

    def zb_end(arr):
        zb_step(arr, 0)
        for half in (0, 1):
            pr, pleft = place(R, half), place(L, half)
            zout[arr, half] = jnp.zeros((128, width), BF)

            def put(*refs):
                total = refs[0][...].astype(F32)
                for ref in refs[1:]:
                    total = total + ref[...].astype(F32)
                zout[arr, half] = total.astype(BF)

            right, left, mine = rbuf.at[arr, R, half, 0], rbuf.at[arr, L, half, 0], outp.at[arr, z]

            @pl.when((myhalf == half) & (pr <= 4) & (pleft <= 4))
            def _():
                put(mine, right, left)

            @pl.when((myhalf == half) & (pr <= 4) & (pleft > 4))
            def _():
                put(mine, right)

            @pl.when((myhalf == half) & (pr > 4) & (pleft <= 4))
            def _():
                put(mine, left)

            @pl.when((myhalf != half) & (pr <= 4))
            def _():
                put(right)

            @pl.when((myhalf != half) & (pleft <= 4))
            def _():
                put(left)

        for k in (2, 1, 3):
            y_copy(arr, k, True).start()
        yback[arr, y] = zout[arr, :, pl.ds(pl.multiple_of(y * 32, 32), 32)]

    def zb_sent(arr):
        for d in (R, L):
            for half in (0, 1):
                p = place(d, half)
                for s in range(1, 6):

                    @pl.when((p >= s) & (p <= 5))
                    def _():
                        rcopy(outp.at[arr, 0], rbuf.at[arr, d, half, s - 1], zb_s.at[arr, d, half, s], zb_r.at[arr, d, half, s - 1], backward[d]).wait_send()

    def x_back(arr):
        for k in (1, 3, 2):
            origin = lax.rem(y + 4 - k, 4)
            wait_in(yback.at[arr, origin], yb_r.at[arr, k])
        rows = jnp.dot(permt[...], yback[arr].reshape(256, width), preferred_element_type=F32).astype(BF)
        xback[arr] = rows.reshape(8, 32, width)
        for kx, kc in order:
            x_copy(arr, kx, kc, True).start()
        eo[arr, me_dp] = xback[arr, me_dp]

    def weight_grad(which):
        def body(i, carry):
            tile = pl.ds(pl.multiple_of(i * 128, 128), 128)
            if which < 2:
                lhs = tokin[0, pl.ds(0, 8), :, tile].reshape(1024, 128)
                rhs = acts[1 + which].reshape(1024, 512)
                out = (ggrad, ugrad)[which]
            else:
                lhs = acts[0, :, :, tile].reshape(1024, 128)
                rhs = tokin[1, pl.ds(0, 8)].reshape(1024, width)
                out = dgrad
            out[tile, :] = lax.dot_general(lhs, rhs, TN, preferred_element_type=F32).astype(BF)
            return carry

        lax.fori_loop(0, width // 128 if which < 2 else 4, body, 0)
        stores[2 + which].start()

    stores = [
        pltpu.make_async_copy(a, b, outsem.at[i])
        for i, (a, b) in enumerate(
            ((mixed, mixed_hbm), (igrad, igrad_hbm), (ggrad, ggrad_hbm), (ugrad, ugrad_hbm), (dgrad, dgrad_hbm))
        )
    ]

    loads[0].wait()
    gather_rows(0)
    loads[1].wait()
    gather_rows(1)
    y_stage(0)
    y_stage(1)
    z_begin(0)
    for s in range(1, 6):
        z_step(0, s)
    z_begin(1)
    loads[2].wait()
    loads[3].wait()
    forward(0)
    z_step(1, 1)
    rs_one(0)
    z_step(1, 2)
    rs_two(0)
    z_step(1, 3)
    rs_end(0)
    activate(0)
    ag_one(0)
    z_step(1, 4)
    ag_two(0)
    z_step(1, 5)
    loads[4].wait()
    forward(1)
    ag_three(0)
    partial_out(0)
    zb_begin(0)
    rs_one(1)
    zb_step(0, 4)
    rs_two(1)
    zb_step(0, 3)
    rs_end(1)
    activate(1)
    ag_one(1)
    zb_step(0, 2)
    ag_two(1)
    zb_step(0, 1)
    ag_three(1)
    partial_out(1)
    zb_begin(1)
    zb_end(0)
    weight_grad(0)
    zb_step(1, 4)
    x_back(0)
    weight_grad(1)
    zb_step(1, 3)
    weight_grad(2)

    x_wait(0, True)
    big = table.astype(BF)
    rest = table - big.astype(F32)
    mid = rest.astype(BF)
    small = (rest - mid.astype(F32)).astype(BF)
    zero = jnp.zeros((128, 128), BF)
    split = jnp.where(lane < 32, big, jnp.where(lane < 64, mid, jnp.where(lane < 96, small, zero)))
    scores = jnp.zeros((128, 32), F32)
    for share in range(8):
        columns = pl.ds(share * width, width)
        outs = eo[0, share]
        mixed[:, columns] = jnp.dot(split, jnp.concatenate([outs] * 4, axis=0), preferred_element_type=F32).astype(BF)
        scores = scores + lax.dot_general(ograd[:, columns], outs, NT, preferred_element_type=F32)
        if share == 3:
            zb_step(1, 2)
    stores[0].start()
    weighted = chosen[:, :32] * scores
    lane8 = lax.broadcasted_iota(jnp.int32, (128, 8), 1)
    pgrad = jnp.zeros((128, 8), F32)
    for k in range(8):
        hit = (ids[:, k : k + 1] == hosted[:, :32]).astype(F32)
        pgrad = pgrad + jnp.where(lane8 == k, jnp.sum(hit * weighted, axis=1, keepdims=True), 0.0)
    pgrad_ref[...] = pgrad

    zb_step(1, 1)
    zb_end(1)
    x_back(1)
    x_wait(1, True)
    chosen_bf = chosen[:, :32].astype(BF)
    for share in range(8):
        igrad[:, pl.ds(share * width, width)] = jnp.dot(chosen_bf, eo[1, share], preferred_element_type=F32).astype(BF)
    stores[1].start()

    for arr in (0, 1):
        for kx, kc in order:
            x_copy(arr, kx, kc, False).wait_send()
            x_copy(arr, kx, kc, True).wait_send()
        for k in (1, 2, 3):
            y_copy(arr, k, False).wait_send()
            y_copy(arr, k, True).wait_send()
        z_sent(arr)
        zb_sent(arr)
    for g in (0, 1):
        c_copy(g).wait_send()
        for copy in rx_copies(g):
            copy.wait_send()
        for k in range(8):
            ag_copy(g, k).wait_send()
    for store in stores:
        store.wait()


def on_device(tokens, out_grad, expert_ids, route_probs, hosted, gate_weight, up_weight, down_weight):
    model_width = tokens.shape[1]
    width, hidden = gate_weight.shape
    slots = jnp.tile(jnp.repeat(hosted, CAP), 4)[None, :]
    vmem = pl.BlockSpec(memory_space=pltpu.VMEM)
    hbm = pl.BlockSpec(memory_space=pl.ANY)
    dma = pltpu.SemaphoreType.DMA
    out = pl.pallas_call(
        functools.partial(kernel, width),
        out_shape=(
            jax.ShapeDtypeStruct(tokens.shape, BF),
            jax.ShapeDtypeStruct(tokens.shape, BF),
            jax.ShapeDtypeStruct(route_probs.shape, F32),
            jax.ShapeDtypeStruct(gate_weight.shape, BF),
            jax.ShapeDtypeStruct(up_weight.shape, BF),
            jax.ShapeDtypeStruct(down_weight.shape, BF),
        ),
        in_specs=[vmem] * 3 + [hbm] * 5,
        out_specs=(hbm, hbm, vmem, hbm, hbm, hbm),
        scratch_shapes=[
            pltpu.VMEM((128, model_width), BF),
            pltpu.VMEM((128, model_width), BF),
            pltpu.VMEM((width, hidden), BF),
            pltpu.VMEM((width, hidden), BF),
            pltpu.VMEM((hidden, width), BF),
            pltpu.VMEM((128, model_width), BF),
            pltpu.VMEM((128, model_width), BF),
            pltpu.VMEM((width, hidden), BF),
            pltpu.VMEM((width, hidden), BF),
            pltpu.VMEM((hidden, width), BF),
            pltpu.VMEM((2, 8, 32, width), BF),
            pltpu.VMEM((2, 8, 32, width), BF),
            pltpu.VMEM((2, 4, 2, 32, width), BF),
            pltpu.VMEM((2, 2, 128, width), BF),
            pltpu.VMEM((2, 10, 128, width), BF),
            pltpu.VMEM((3, 4, 2, 128, hidden), F32),
            pltpu.VMEM((3, 4, 128, hidden), F32),
            pltpu.VMEM((2, 3, 128, hidden // 2), F32),
            pltpu.VMEM((4, 3, 128, hidden // 2), F32),
            pltpu.VMEM((3, 128, hidden), F32),
            pltpu.VMEM((3, 8, 128, hidden), BF),
            pltpu.VMEM((2, 8, 128, width), BF),
            pltpu.VMEM((2, 2, 2, 5, 128, width), BF),
            pltpu.VMEM((2, 2, 128, width), BF),
            pltpu.VMEM((2, 4, 2, 32, width), BF),
            pltpu.VMEM((2, 8, 32, width), BF),
            pltpu.VMEM((2, 8, 32, width), BF),
            pltpu.VMEM((256, 256), BF),
            pltpu.VMEM((256, 256), BF),
            dma((5,)), dma((5,)),
            dma((2, 8)), dma((2, 8)), dma((2, 4)), dma((2, 4)),
            dma((2, 2, 2, 5)), dma((2, 2, 2, 6)),
            dma((2,)), dma((2,)), dma((2, 6)), dma((2, 6)), dma((2, 8)), dma((2, 8)),
            dma((2, 2, 2, 6)), dma((2, 2, 2, 5)), dma((2, 4)), dma((2, 4)), dma((2, 8)), dma((2, 8)),
        ],
        compiler_params=pltpu.CompilerParams(
            collective_id=0, has_side_effects=True, vmem_limit_bytes=60 * 1024 * 1024
        ),
        cost_estimate=pl.CostEstimate(flops=9 * 2 * 1024 * 896 * 512, bytes_accessed=16_000_000, transcendentals=65536),
    )(expert_ids, route_probs, slots, tokens, out_grad, gate_weight, up_weight, down_weight)
    return tuple(out)


def solution(mesh):
    return jax.shard_map(
        on_device,
        mesh=mesh,
        in_specs=(
            P(("dp", "expert"), None),
            P(("dp", "expert"), None),
            P(("dp", "expert"), None),
            P(("dp", "expert"), None),
            P(),
            P("dp", "expert"),
            P("dp", "expert"),
            P("expert", "dp"),
        ),
        out_specs=(
            P(("dp", "expert"), None),
            P(("dp", "expert"), None),
            P(("dp", "expert"), None),
            P("dp", "expert"),
            P("dp", "expert"),
            P("expert", "dp"),
        ),
        check_vma=False,
    )
```

```python
import functools

import jax
import jax.numpy as jnp
from jax import lax
from jax.experimental import pallas as pl
from jax.experimental.pallas import tpu as pltpu
from jax.sharding import PartitionSpec as P

BF = jnp.bfloat16
F32 = jnp.float32
MESH = pl.DeviceIdType.MESH
NT = (((1,), (1,)), ((), ()))
TN = (((0,), (0,)), ((), ()))
R, L = 0, 1


def kernel(
    width,
    ids_ref, probs_ref, hosted_ref, tokens_hbm, ograd_hbm, wg_hbm, wu_hbm, wd_hbm,
    mixed_hbm, pgrad_ref, ggrad_hbm, ugrad_hbm, dgrad_hbm, back_hbm, select_ref,
    tokens, ograd, wg, wu, wd, mixed, ggrad, ugrad, dgrad,
    xsend, xbuf, ysend, zsrc, tokin,
    part, rs, xr1, fin, own, acts,
    outp, rbuf, zout, yback, xback, eo, perm, permt,
    insem, outsem, xs_s, xs_r, ys_s, ys_r, zs_s, zs_r,
    cx_s, cx_r, rx_s, rx_r, ag_s, ag_r,
    zb_s, zb_r, yb_s, yb_r, xb_s, xb_r,
):
    me_dp = lax.axis_index("dp")
    me_e = lax.axis_index("expert")
    x, c = lax.div(me_dp, 2), lax.rem(me_dp, 2)
    y, z = lax.div(me_e, 8), lax.rem(me_e, 8)
    myhalf = lax.div(z, 4)

    def dev(x_, c_, y_, z_):
        return (x_ * 2 + c_, y_ * 8 + z_)

    def rcopy(src, dst, ssem, rsem, where):
        return pltpu.make_async_remote_copy(
            src_ref=src, dst_ref=dst, send_sem=ssem, recv_sem=rsem,
            device_id=where, device_id_type=MESH,
        )

    other_core = dev(x, 1 - c, y, z)
    xr_dev = dev(lax.rem(x + 1, 4), c, y, z)
    xl_dev = dev(lax.rem(x + 3, 4), c, y, z)

    def wait_in(dst, rsem):
        rcopy(dst, dst, rsem, rsem, other_core).wait_recv()

    loads = [
        pltpu.make_async_copy(a, b, insem.at[i])
        for i, (a, b) in enumerate(
            ((tokens_hbm, tokens), (ograd_hbm, ograd), (wg_hbm, wg), (wu_hbm, wu), (wd_hbm, wd))
        )
    ]
    for load in loads:
        load.start()
    stores = [
        pltpu.make_async_copy(a, b, outsem.at[i])
        for i, (a, b) in enumerate(
            ((mixed, mixed_hbm), (ggrad, ggrad_hbm), (ugrad, ugrad_hbm), (dgrad, dgrad_hbm), (eo.at[1], back_hbm))
        )
    ]

    barrier = pltpu.get_barrier_semaphore()
    partners = []
    for kx in range(4):
        for kc in range(2):
            if kx or kc:
                partners.append(dev(lax.rem(x + kx, 4), lax.rem(c + kc, 2), y, z))
    for k in range(1, 4):
        partners.append(dev(x, c, lax.rem(y + k, 4), z))
    partners += [dev(x, c, y, lax.rem(z + 1, 8)), dev(x, c, y, lax.rem(z + 7, 8))]
    for partner in partners:
        pl.semaphore_signal(barrier, inc=1, device_id=partner, device_id_type=MESH)

    row = lax.broadcasted_iota(jnp.int32, (128, 128), 0)
    lane = lax.broadcasted_iota(jnp.int32, (128, 128), 1)
    ids = ids_ref[...]
    probs = probs_ref[...]
    expert_of = (row >> 1) & 7
    hosted = jnp.zeros((128, 128), jnp.int32)
    for w in range(8):
        hosted = jnp.where(expert_of == w, hosted_ref[w], hosted)
    matched = jnp.zeros((128, 128), F32)
    prob_at = jnp.zeros((128, 128), F32)
    for k in range(8):
        hit = (ids[k : k + 1, :] == hosted).astype(F32)
        matched = matched + hit
        prob_at = prob_at + hit * probs[k : k + 1, :]
    before = (row < lane).astype(BF)
    rank = jnp.dot(matched.astype(BF), before, preferred_element_type=F32)
    cap_of = ((row >> 4) & 1) * 2 + (row & 1)
    chosen = matched * (rank == cap_of.astype(F32)).astype(F32)
    table = prob_at * chosen
    select = chosen[:32].astype(BF)
    slot_prob = jnp.sum(table[:32], axis=1, keepdims=True)
    select_ref[...] = select

    def moved(q):
        return ((q >> 1) & 7) * 16 + (q >> 5) * 4 + ((q >> 4) & 1) * 2 + (q & 1)

    perm[...] = (lane == moved(row)).astype(BF)
    permt[...] = (row == moved(lane)).astype(BF)

    def x_copy(arr, q, k, back):
        xd, cd = lax.rem(x + lax.div(k, 2), 4), lax.rem(c + lax.rem(k, 2), 2)
        there = xd * 2 + cd
        if back:
            return rcopy(xback.at[arr, q, there], eo.at[arr, me_dp, pl.ds(q * 16, 16)], xb_s.at[arr, q], xb_r.at[arr, q], dev(xd, cd, y, z))
        return rcopy(xsend.at[arr, q, there], xbuf.at[arr, q, me_dp], xs_s.at[arr, q], xs_r.at[arr, q], dev(xd, cd, y, z))

    def x_send(arr, q, back):
        def body(i, carry):
            x_copy(arr, q, lax.rem(i + 3, 7) + 1, back).start()
            return carry

        lax.fori_loop(0, 7, body, 0)

    def x_wait(arr, q, back):
        wait_in(eo.at[arr, pl.ds(0, 7), pl.ds(q * 16, 16)] if back else xbuf.at[arr, q, pl.ds(0, 7)], (xb_r if back else xs_r).at[arr, q])

    def wait_out(src, ssem):
        rcopy(src, src, ssem, ssem, other_core).wait_send()

    def gather_rows(arr):
        def body(index, carry):
            columns = pl.ds(pl.multiple_of(index * width, 128), width)
            source = tokens if arr == 0 else ograd
            rows = jnp.dot(select, source[:, columns], preferred_element_type=F32)
            if arr == 1:
                rows = slot_prob * rows
            rows = rows.astype(BF)
            for q in (0, 1):
                xsend[arr, q, index] = rows[q * 16 : q * 16 + 16]
            return carry

        lax.fori_loop(0, 8, body, 0)
        for q in (0, 1):
            xbuf[arr, q, me_dp] = xsend[arr, q, me_dp]

    def y_copy(arr, q, k, back):
        yd = lax.rem(y + k, 4)
        if back:
            src = zout.at[arr, q, :, pl.ds(pl.multiple_of(yd * 16, 16), 16)]
            return rcopy(src, yback.at[arr, q, y], yb_s.at[arr, q], yb_r.at[arr, q], dev(x, c, yd, z))
        dst = zsrc.at[arr, q, :, pl.ds(pl.multiple_of(y * 16, 16), 16)]
        return rcopy(ysend.at[arr, q, yd], dst, ys_s.at[arr, q], ys_r.at[arr, q], dev(x, c, yd, z))

    def y_stage(arr, q):
        x_wait(arr, q, False)
        rows = jnp.dot(perm[...], xbuf[arr, q].reshape(128, width), preferred_element_type=F32).astype(BF)
        ysend[arr, q] = rows.reshape(4, 2, 16, width)
        for k in (2, 1, 3):
            y_copy(arr, q, k, False).start()
        mine = pl.ds(pl.multiple_of(y * 16, 16), 16)
        zsrc[arr, q, :, mine] = ysend[arr, q, y]

    def y_wait(arr, q):
        wait_in(zsrc.at[arr, q, :, pl.ds(0, 48)], ys_r.at[arr, q])

    right0, left0 = lax.rem(z + 2, 8), lax.rem(13 - z, 8)

    def each_line(body):
        def line(i, carry):
            d, half = lax.div(i, 2), lax.rem(i, 2)
            body(d, half, lax.rem(right0 + d * (left0 + 8 - right0) + 4 * half, 8))
            return carry

        lax.fori_loop(0, 4, line, 0)

    def origin_z(d, s):
        return lax.rem(z + 8 - (1 - 2 * d) * s, 8)

    def z_dev(d, back):
        step = (2 * d - 1) if back else (1 - 2 * d)
        return dev(x, c, y, lax.rem(z + 8 + step, 8))

    def is_zero(p):
        return lax.div(7 - p, 7)

    def is_one(p):
        return is_zero(lax.rem(p + 7, 8))

    def z_send(arr, q, d, half, p, s):
        src = origin_z(d, s)
        if s == 0:
            first = is_zero(p)
            slot = src + first * (8 + d - src)
            rcopy(zsrc.at[arr, q, half], tokin.at[arr, q, slot], zs_s.at[arr, q, d, half], zs_r.at[arr, q, d, 1 - first], z_dev(d, False)).start()
        else:
            came = src + is_one(p) * (8 + d - src) if s == 1 else src
            rcopy(tokin.at[arr, q, came], tokin.at[arr, q, src], zs_s.at[arr, q, d, half], zs_r.at[arr, q, d, s + 1], z_dev(d, False)).start()

    def z_sent(arr, q):
        def body(d, half, p):
            for last in range(5):

                @pl.when(p == last)
                def _():
                    wait_out(tokin.at[arr, q, pl.ds(0, last + 1)], zs_s.at[arr, q, d, half])

        each_line(body)

    def z_step(arr, q, s):
        def body(d, half, p):
            @pl.when((p >= s) & (p <= 5))
            def _():
                src = origin_z(d, s)
                transit = is_one(p) if s == 1 else 0
                wait_in(tokin.at[arr, q, src + transit * (8 + d - src)], zs_r.at[arr, q, d, s * (1 - transit)])
                if s < 5:

                    @pl.when(p <= 4)
                    def _():
                        z_send(arr, q, d, half, p, s)

        each_line(body)

    def z_begin(arr, q):
        y_wait(arr, q)
        for far in (True, False):

            def body(d, half, p):
                @pl.when(p < 4 if far else p == 4)
                def _():
                    z_send(arr, q, d, half, p, 0)

            each_line(body)
        tokin[arr, q, z] = zsrc[arr, q, myhalf]

    def forward(arr, q):
        def body(i, carry):
            rows = tokin[arr, q, pl.ds(4 * i, 4)].reshape(256, width)
            two = pl.ds(2 * i, 2)
            if arr == 0:
                part[0, q, two] = jnp.dot(rows, wg[...], preferred_element_type=F32).reshape(2, 2, 64, 512)
                part[1, q, two] = jnp.dot(rows, wu[...], preferred_element_type=F32).reshape(2, 2, 64, 512)
            else:
                part[2, q, two] = lax.dot_general(rows, wd[...], NT, preferred_element_type=F32).reshape(2, 2, 64, 512)
            return carry

        lax.fori_loop(0, 2, body, 0)
        c_copy(arr, q).start()

    kinds = (pl.ds(0, 2), pl.ds(2, 1))
    which = ((0, 1), (2,))

    def c_copy(g, q):
        return rcopy(part.at[kinds[g], q, :, 1 - c], rs.at[kinds[g], q], cx_s.at[g, q], cx_r.at[g, q], other_core)

    low, high = pl.ds(0, 256), pl.ds(256, 256)
    ahead, behind, across = lax.rem(x + 1, 4), lax.rem(x + 3, 4), lax.rem(x + 2, 4)

    def rx_copies(g, q):
        ks = kinds[g]
        return [
            rcopy(src, dst, rx_s.at[g, q], rx_r.at[g, q, min(k, 2)], to)
            for k, (src, dst, to) in enumerate((
                (rs.at[ks, q, across, :, low], xr1.at[R, ks, q], xr_dev),
                (rs.at[ks, q, across, :, high], xr1.at[L, ks, q], xl_dev),
                (rs.at[ks, q, ahead, :, high], fin.at[0, ks, q], xr_dev),
                (rs.at[ks, q, behind, :, low], fin.at[1, ks, q], xl_dev),
                (xr1.at[R, ks, q], fin.at[2, ks, q], xr_dev),
                (xr1.at[L, ks, q], fin.at[3, ks, q], xl_dev),
            ))
        ]

    def rs_one(g, q):
        c_copy(g, q).wait_recv()
        copies = rx_copies(g, q)

        def add(chunk):
            for j in which[g]:
                rs[j, q, chunk] = part[j, q, chunk, c] + rs[j, q, chunk]

        add(across)
        copies[0].start()
        copies[1].start()
        add(ahead)
        copies[2].start()
        add(behind)
        copies[3].start()
        add(x)

    def rs_two(g, q):
        copies = rx_copies(g, q)
        copies[0].wait_recv()
        for j in which[g]:
            xr1[R, j, q] = xr1[R, j, q] + rs[j, q, ahead, :, low]
        copies[4].start()
        copies[1].wait_recv()
        for j in which[g]:
            xr1[L, j, q] = xr1[L, j, q] + rs[j, q, behind, :, high]
        copies[5].start()

    def rs_end(g, q):
        wait_in(fin.at[:, kinds[g], q], rx_r.at[g, q, 2])
        for j in which[g]:
            own[j, q, :, low] = rs[j, q, x, :, low] + fin[1, j, q] + fin[2, j, q]
            own[j, q, :, high] = rs[j, q, x, :, high] + fin[0, j, q] + fin[3, j, q]
        gate = own[0, q]
        up = own[1, q]
        sig = jax.nn.sigmoid(gate)
        silu = gate * sig
        if g == 0:
            acts[0, q, me_dp] = (silu * up).astype(BF)
        else:
            back = own[2, q]
            acts[1, q, me_dp] = (back * up * sig * (1.0 + gate * (1.0 - sig))).astype(BF)
            acts[2, q, me_dp] = (back * silu).astype(BF)
        for k in range(3):
            ag_copy(g, q, k).start()

    held = (pl.ds(0, 1), pl.ds(1, 2))

    def ag_copy(g, q, k):
        ks = held[g]
        before_me, after_me, far = behind * 2 + c, ahead * 2 + c, across * 2 + c
        what, where = (
            (acts.at[ks, q, me_dp], xr_dev),
            (acts.at[ks, q, me_dp], xl_dev),
            (acts.at[ks, q, me_dp], other_core),
            (acts.at[ks, q, before_me, :, low], xr_dev),
            (acts.at[ks, q, after_me, :, high], xl_dev),
            (acts.at[ks, q, before_me], other_core),
            (acts.at[ks, q, after_me], other_core),
            (acts.at[ks, q, far], other_core),
        )[k]
        return rcopy(what, what, ag_s.at[g, q], ag_r.at[g, q, (0, 1, 3, 2, 2, 3, 3, 3)[k]], where)

    def ag_wait(g, q, k):
        ks = held[g]
        dst = (
            acts.at[ks, q, behind * 2 + c],
            acts.at[ks, q, ahead * 2 + c],
            acts.at[ks, q, across * 2 + c],
            acts.at[ks, q, pl.ds(0, 4)],
        )[k]
        wait_in(dst, ag_r.at[g, q, k])

    def ag_two(g, q):
        ag_wait(g, q, 0)
        ag_copy(g, q, 3).start()
        ag_copy(g, q, 5).start()
        ag_wait(g, q, 1)
        ag_copy(g, q, 4).start()
        ag_copy(g, q, 6).start()

    def ag_three(g, q):
        ag_wait(g, q, 2)
        ag_copy(g, q, 7).start()
        ag_wait(g, q, 3)

    def partial_out(arr, q):
        def body(i, carry):
            four = pl.ds(4 * i, 4)
            if arr == 0:
                piece = jnp.dot(acts[0, q, four].reshape(256, 512), wd[...], preferred_element_type=F32)
            else:
                piece = lax.dot_general(acts[1, q, four].reshape(256, 512), wg[...], NT, preferred_element_type=F32)
                piece = piece + lax.dot_general(acts[2, q, four].reshape(256, 512), wu[...], NT, preferred_element_type=F32)
            outp[arr, q, four] = piece.astype(BF).reshape(4, 64, width)
            return carry

        lax.fori_loop(0, 2, body, 0)
        zb_begin(arr, q)

    def zb_copy(arr, q, d, half, p, s, whole):
        src = outp.at[arr, q, origin_z(d, s)] if whole else rbuf.at[arr, q, d, half, s]
        sem = s - 1
        if s == 1:
            sem = 5 * is_one(p)
        return rcopy(src, rbuf.at[arr, q, d, half, s - 1], zb_s.at[arr, q, d, half], zb_r.at[arr, q, d, sem], z_dev(d, True))

    def zb_begin(arr, q):
        def body(d, half, p):
            @pl.when(p == 5)
            def _():
                for s in (5, 4, 3, 2, 1):
                    zb_copy(arr, q, d, half, p, s, True).start()

        each_line(body)

    def zb_step(arr, q, s):
        def body(d, half, p):
            @pl.when((p >= s) & (p <= 4))
            def _():
                sem = s
                if s == 0:
                    sem = 5 * is_zero(p)
                wait_in(rbuf.at[arr, q, d, half, s], zb_r.at[arr, q, d, sem])
                if s > 0:

                    @pl.when(p >= 2)
                    def _():
                        total = rbuf[arr, q, d, half, s].astype(F32) + outp[arr, q, origin_z(d, s)].astype(F32)
                        rbuf[arr, q, d, half, s] = total.astype(BF)

                    zb_copy(arr, q, d, half, p, s, False).start()

        each_line(body)

    def zb_end(arr, q):
        zb_step(arr, q, 0)
        for half in (0, 1):
            pr, pleft = lax.rem(right0 + 4 * half, 8), lax.rem(left0 + 4 * half, 8)

            def put(*refs):
                total = refs[0][...].astype(F32)
                for ref in refs[1:]:
                    total = total + ref[...].astype(F32)
                zout[arr, q, half] = total.astype(BF)

            right, left, mine = rbuf.at[arr, q, R, half, 0], rbuf.at[arr, q, L, half, 0], outp.at[arr, q, z]

            @pl.when((myhalf == half) & (pr <= 4) & (pleft <= 4))
            def _():
                put(mine, right, left)

            @pl.when((myhalf == half) & (pr <= 4) & (pleft > 4))
            def _():
                put(mine, right)

            @pl.when((myhalf == half) & (pr > 4) & (pleft <= 4))
            def _():
                put(mine, left)

            @pl.when((myhalf != half) & (pr <= 4))
            def _():
                put(right)

            @pl.when((myhalf != half) & (pleft <= 4))
            def _():
                put(left)

        for k in (2, 1, 3):
            y_copy(arr, q, k, True).start()
        yback[arr, q, y] = zout[arr, q, :, pl.ds(pl.multiple_of(y * 16, 16), 16)]

    def zb_sent(arr, q):
        def body(d, half, p):
            for last in range(1, 6):

                @pl.when(p == last)
                def _():
                    wait_out(outp.at[arr, q, pl.ds(0, last)], zb_s.at[arr, q, d, half])

        each_line(body)

    def x_back(arr, q):
        wait_in(yback.at[arr, q, pl.ds(0, 3)], yb_r.at[arr, q])
        rows = jnp.dot(permt[...], yback[arr, q].reshape(128, width), preferred_element_type=F32).astype(BF)
        xback[arr, q] = rows.reshape(8, 16, width)
        x_send(arr, q, True)
        eo[arr, me_dp, pl.ds(q * 16, 16)] = xback[arr, q, me_dp]

    def weight_grad(kind):
        def body(i, carry):
            tile = pl.ds(pl.multiple_of(i * 128, 128), 128)
            total = jnp.zeros((128, 512 if kind < 2 else width), F32)
            for q in (0, 1):
                if kind < 2:
                    lhs = tokin[0, q, pl.ds(0, 8), :, tile].reshape(512, 128)
                    rhs = acts[1 + kind, q].reshape(512, 512)
                else:
                    lhs = acts[0, q, :, :, tile].reshape(512, 128)
                    rhs = tokin[1, q, pl.ds(0, 8)].reshape(512, width)
                total = total + lax.dot_general(lhs, rhs, TN, preferred_element_type=F32)
            (ggrad, ugrad, dgrad)[kind][tile, :] = total.astype(BF)
            return carry

        lax.fori_loop(0, width // 128 if kind < 2 else 4, body, 0)
        stores[1 + kind].start()

    def token_side():
        x_wait(0, 0, True)
        x_wait(0, 1, True)
        big = table.astype(BF).astype(F32)
        rest = table - big
        mid = rest.astype(BF).astype(F32)
        small = (rest - mid).astype(BF).astype(F32)
        split = jnp.where(row < 32, big, jnp.where(row < 64, mid, jnp.where(row < 96, small, 0.0))).T.astype(BF)

        def body(share, scores):
            columns = pl.ds(pl.multiple_of(share * width, 128), width)
            outs = eo[0, share]
            mixed[:, columns] = jnp.dot(split, jnp.concatenate([outs] * 4, axis=0), preferred_element_type=F32).astype(BF)
            return scores + lax.dot_general(outs, ograd[:, columns], NT, preferred_element_type=F32)

        scores = lax.fori_loop(0, 8, body, jnp.zeros((32, 128), F32))
        stores[0].start()
        weighted = chosen[:32] * scores
        for k in range(8):
            hit = (ids[k : k + 1, :] == hosted[:32]).astype(F32)
            pgrad_ref[k : k + 1, :] = jnp.sum(hit * weighted, axis=0, keepdims=True)

    def sent_mid(g, q):
        c_copy(g, q).wait_send()
        wait_out(rs.at[kinds[g], q, pl.ds(0, 3)], rx_s.at[g, q])
        wait_out(acts.at[held[g], q, pl.ds(0, 7)], ag_s.at[g, q])

    def sent_in(arr, q):
        wait_out(xsend.at[arr, q, pl.ds(0, 7)], xs_s.at[arr, q])
        wait_out(ysend.at[arr, q, pl.ds(0, 3)], ys_s.at[arr, q])
        z_sent(arr, q)

    def sent_out(arr, q):
        zb_sent(arr, q)
        wait_out(zout.at[arr, q, :, pl.ds(0, 48)], yb_s.at[arr, q])
        wait_out(xback.at[arr, q, pl.ds(0, 7)], xb_s.at[arr, q])

    T, G = 0, 1
    loads[0].wait()
    gather_rows(T)
    pl.semaphore_wait(barrier, len(partners))
    x_send(T, 0, False)
    x_send(T, 1, False)
    loads[1].wait()
    gather_rows(G)
    y_stage(T, 0)
    x_send(G, 0, False)
    x_send(G, 1, False)
    y_stage(T, 1)
    z_begin(T, 0)
    y_stage(G, 0)
    z_step(T, 0, 1)
    z_begin(T, 1)
    y_stage(G, 1)
    z_step(T, 0, 2)
    z_step(T, 1, 1)
    z_step(T, 0, 3)
    z_step(T, 1, 2)
    z_step(T, 0, 4)
    z_step(T, 1, 3)
    z_begin(G, 0)
    z_step(T, 0, 5)
    for load in loads[2:]:
        load.wait()
    forward(T, 0)
    z_step(T, 1, 4)
    z_step(G, 0, 1)
    z_step(T, 1, 5)
    z_begin(G, 1)
    forward(T, 1)
    z_step(G, 0, 2)
    rs_one(T, 0)
    z_step(G, 1, 1)
    z_step(G, 0, 3)
    rs_two(T, 0)
    rs_one(T, 1)
    z_step(G, 1, 2)
    z_step(G, 0, 4)
    rs_end(T, 0)
    rs_two(T, 1)
    z_step(G, 1, 3)
    z_step(G, 0, 5)
    forward(G, 0)
    ag_two(T, 0)
    rs_end(T, 1)
    z_step(G, 1, 4)
    ag_three(T, 0)
    partial_out(T, 0)
    ag_two(T, 1)
    rs_one(G, 0)
    z_step(G, 1, 5)
    forward(G, 1)
    zb_step(T, 0, 4)
    ag_three(T, 1)
    partial_out(T, 1)
    rs_two(G, 0)
    zb_step(T, 0, 3)
    rs_one(G, 1)
    zb_step(T, 1, 4)
    rs_end(G, 0)
    zb_step(T, 0, 2)
    rs_two(G, 1)
    zb_step(T, 1, 3)
    ag_two(G, 0)
    zb_step(T, 0, 1)
    rs_end(G, 1)
    zb_step(T, 1, 2)
    ag_three(G, 0)
    partial_out(G, 0)
    zb_end(T, 0)
    ag_two(G, 1)
    zb_step(T, 1, 1)
    zb_step(G, 0, 4)
    ag_three(G, 1)
    partial_out(G, 1)
    zb_end(T, 1)
    zb_step(G, 0, 3)
    x_back(T, 0)
    weight_grad(0)
    zb_step(G, 1, 4)
    zb_step(G, 0, 2)
    x_back(T, 1)
    weight_grad(1)
    zb_step(G, 1, 3)
    zb_step(G, 0, 1)
    weight_grad(2)
    zb_step(G, 1, 2)
    zb_end(G, 0)
    token_side()
    zb_step(G, 1, 1)
    x_back(G, 0)
    zb_end(G, 1)
    for arr in (T, G):
        for q in (0, 1):
            sent_in(arr, q)
            sent_mid(arr, q)
    for arr, q in ((T, 0), (T, 1), (G, 0)):
        sent_out(arr, q)
    x_back(G, 1)
    x_wait(G, 0, True)
    x_wait(G, 1, True)
    stores[4].start()
    sent_out(G, 1)
    for store in stores:
        store.wait()


def finish(width, mixed_in, ggrad_in, ugrad_in, dgrad_in, back, select, pgrad_in, mixed, igrad, pgrad, ggrad, ugrad, dgrad, held, gbuf, ubuf, dbuf, tile, isem, osem, tsem):
    moves = []
    for i in range(4):
        rows = pl.ds(i * 32, 32)
        moves.append((mixed_in.at[rows], held.at[rows], mixed.at[rows]))
    moves += [(ggrad_in, gbuf, ggrad), (ugrad_in, ubuf, ugrad), (dgrad_in, dbuf, dgrad)]
    come = [pltpu.make_async_copy(a, b, isem.at[i]) for i, (a, b, _) in enumerate(moves)]
    leave = [pltpu.make_async_copy(b, o, osem.at[i]) for i, (_, b, o) in enumerate(moves)]
    for move in come:
        move.start()
    pgrad[...] = pgrad_in[...]
    outs = []
    for share in range(8):
        columns = pl.ds(share * width, width)
        tile[:, columns] = lax.dot_general(select[...], back[share], TN, preferred_element_type=F32).astype(BF)
        outs.append(pltpu.make_async_copy(tile.at[:, columns], igrad.at[:, columns], tsem.at[share]))
        outs[-1].start()
        if share < 7:
            come[share].wait()
            leave[share].start()
    for out in outs + leave:
        out.wait()


def on_device(tokens, out_grad, expert_ids, route_probs, hosted, gate_weight, up_weight, down_weight):
    model_width = tokens.shape[1]
    width, hidden = gate_weight.shape
    vmem = pl.BlockSpec(memory_space=pltpu.VMEM)
    smem = pl.BlockSpec(memory_space=pltpu.SMEM)
    hbm = pl.BlockSpec(memory_space=pl.ANY)
    dma = pltpu.SemaphoreType.DMA
    row_shape = jax.ShapeDtypeStruct(tokens.shape, BF)
    side_shape = jax.ShapeDtypeStruct((8, 128), F32)
    grads = (
        jax.ShapeDtypeStruct(gate_weight.shape, BF),
        jax.ShapeDtypeStruct(up_weight.shape, BF),
        jax.ShapeDtypeStruct(down_weight.shape, BF),
    )
    mixed, pgrad, ggrad, ugrad, dgrad, back, select = pl.pallas_call(
        functools.partial(kernel, width),
        out_shape=(
            row_shape, side_shape, *grads,
            jax.ShapeDtypeStruct((8, 32, width), BF),
            jax.ShapeDtypeStruct((32, 128), BF),
        ),
        in_specs=[vmem, vmem, smem] + [hbm] * 5,
        out_specs=(hbm, vmem, hbm, hbm, hbm, hbm, vmem),
        scratch_shapes=[
            pltpu.VMEM((128, model_width), BF),
            pltpu.VMEM((128, model_width), BF),
            pltpu.VMEM((width, hidden), BF),
            pltpu.VMEM((width, hidden), BF),
            pltpu.VMEM((hidden, width), BF),
            pltpu.VMEM((128, model_width), BF),
            pltpu.VMEM((width, hidden), BF),
            pltpu.VMEM((width, hidden), BF),
            pltpu.VMEM((hidden, width), BF),
            pltpu.VMEM((2, 2, 8, 16, width), BF),
            pltpu.VMEM((2, 2, 8, 16, width), BF),
            pltpu.VMEM((2, 2, 4, 2, 16, width), BF),
            pltpu.VMEM((2, 2, 2, 64, width), BF),
            pltpu.VMEM((2, 2, 10, 64, width), BF),
            pltpu.VMEM((3, 2, 4, 2, 64, hidden), F32),
            pltpu.VMEM((3, 2, 4, 64, hidden), F32),
            pltpu.VMEM((2, 3, 2, 64, hidden // 2), F32),
            pltpu.VMEM((4, 3, 2, 64, hidden // 2), F32),
            pltpu.VMEM((3, 2, 64, hidden), F32),
            pltpu.VMEM((3, 2, 8, 64, hidden), BF),
            pltpu.VMEM((2, 2, 8, 64, width), BF),
            pltpu.VMEM((2, 2, 2, 2, 5, 64, width), BF),
            pltpu.VMEM((2, 2, 2, 64, width), BF),
            pltpu.VMEM((2, 2, 4, 2, 16, width), BF),
            pltpu.VMEM((2, 2, 8, 16, width), BF),
            pltpu.VMEM((2, 8, 32, width), BF),
            pltpu.VMEM((128, 128), BF),
            pltpu.VMEM((128, 128), BF),
            dma((5,)), dma((5,)),
            dma((2, 2)), dma((2, 2)), dma((2, 2)), dma((2, 2)),
            dma((2, 2, 2, 2)), dma((2, 2, 2, 6)),
            dma((2, 2)), dma((2, 2)), dma((2, 2)), dma((2, 2, 3)), dma((2, 2)), dma((2, 2, 4)),
            dma((2, 2, 2, 2)), dma((2, 2, 2, 6)), dma((2, 2)), dma((2, 2)), dma((2, 2)), dma((2, 2)),
        ],
        compiler_params=pltpu.CompilerParams(
            collective_id=0, has_side_effects=True, vmem_limit_bytes=60 * 1024 * 1024
        ),
        cost_estimate=pl.CostEstimate(flops=9 * 2 * 1024 * 896 * 512, bytes_accessed=16_000_000, transcendentals=65536),
    )(expert_ids.T, route_probs.T, hosted, tokens, out_grad, gate_weight, up_weight, down_weight)
    mixed, igrad, pgrad, ggrad, ugrad, dgrad = pl.pallas_call(
        functools.partial(finish, width),
        out_shape=(row_shape, row_shape, side_shape, *grads),
        in_specs=[hbm] * 4 + [vmem] * 3,
        out_specs=(hbm, hbm, vmem, hbm, hbm, hbm),
        scratch_shapes=[
            pltpu.VMEM((128, model_width), BF),
            pltpu.VMEM((width, hidden), BF),
            pltpu.VMEM((width, hidden), BF),
            pltpu.VMEM((hidden, width), BF),
            pltpu.VMEM((128, model_width), BF),
            dma((7,)), dma((7,)), dma((8,)),
        ],
        compiler_params=pltpu.CompilerParams(vmem_limit_bytes=60 * 1024 * 1024),
    )(mixed, ggrad, ugrad, dgrad, back, select, pgrad)
    return mixed, igrad, pgrad.T, ggrad, ugrad, dgrad


def solution(mesh):
    return jax.shard_map(
        on_device,
        mesh=mesh,
        in_specs=(
            P(("dp", "expert"), None),
            P(("dp", "expert"), None),
            P(("dp", "expert"), None),
            P(("dp", "expert"), None),
            P(),
            P("dp", "expert"),
            P("dp", "expert"),
            P("expert", "dp"),
        ),
        out_specs=(
            P(("dp", "expert"), None),
            P(("dp", "expert"), None),
            P(("dp", "expert"), None),
            P("dp", "expert"),
            P("dp", "expert"),
            P("expert", "dp"),
        ),
        check_vma=False,
    )
```

```python
import functools

import jax
import jax.numpy as jnp
from jax import lax
from jax.experimental import pallas as pl
from jax.experimental.pallas import tpu as pltpu
from jax.sharding import PartitionSpec as P

BF = jnp.bfloat16
F32 = jnp.float32
MESH = pl.DeviceIdType.MESH
NT = (((1,), (1,)), ((), ()))
TN = (((0,), (0,)), ((), ()))
R, L = 0, 1


def kernel(
    width,
    ids_ref, probs_ref, hosted_ref, tokens_hbm, ograd_hbm, wg_hbm, wu_hbm, wd_hbm,
    mixed_hbm, pgrad_ref, ggrad_hbm, ugrad_hbm, dgrad_hbm, back_hbm, select_ref,
    tokens, ograd, wg, wu, wd, mixed, ggrad, ugrad, dgrad,
    xsend, xbuf, ysend, zsrc, tokin,
    part, rs, xr1, fin, own, acts,
    outp, rbuf, zout, yback, xback, eo, perm, permt,
    insem, outsem, xs_s, xs_r, ys_s, ys_r, zs_s, zs_r,
    cx_s, cx_r, rx_s, rx_r, ag_s, ag_r,
    zb_s, zb_r, yb_s, yb_r, xb_s, xb_r,
):
    me_dp = lax.axis_index("dp")
    me_e = lax.axis_index("expert")
    x, c = lax.div(me_dp, 2), lax.rem(me_dp, 2)
    y, z = lax.div(me_e, 8), lax.rem(me_e, 8)
    myhalf = lax.div(z, 4)

    def dev(x_, c_, y_, z_):
        return (x_ * 2 + c_, y_ * 8 + z_)

    def rcopy(src, dst, ssem, rsem, where):
        return pltpu.make_async_remote_copy(
            src_ref=src, dst_ref=dst, send_sem=ssem, recv_sem=rsem,
            device_id=where, device_id_type=MESH,
        )

    other_core = dev(x, 1 - c, y, z)
    xr_dev = dev(lax.rem(x + 1, 4), c, y, z)
    xl_dev = dev(lax.rem(x + 3, 4), c, y, z)

    def wait_in(dst, rsem):
        rcopy(dst, dst, rsem, rsem, other_core).wait_recv()

    loads = [
        pltpu.make_async_copy(a, b, insem.at[i])
        for i, (a, b) in enumerate(
            ((tokens_hbm, tokens), (ograd_hbm, ograd), (wg_hbm, wg), (wu_hbm, wu), (wd_hbm, wd))
        )
    ]
    for load in loads:
        load.start()
    stores = [
        pltpu.make_async_copy(a, b, outsem.at[i])
        for i, (a, b) in enumerate(
            ((mixed, mixed_hbm), (ggrad, ggrad_hbm), (ugrad, ugrad_hbm), (dgrad, dgrad_hbm), (eo.at[1], back_hbm))
        )
    ]

    barrier = pltpu.get_barrier_semaphore()
    partners = []
    for kx in range(4):
        for kc in range(2):
            if kx or kc:
                partners.append(dev(lax.rem(x + kx, 4), lax.rem(c + kc, 2), y, z))
    for k in range(1, 4):
        partners.append(dev(x, c, lax.rem(y + k, 4), z))
    partners += [dev(x, c, y, lax.rem(z + 1, 8)), dev(x, c, y, lax.rem(z + 7, 8))]
    for partner in partners:
        pl.semaphore_signal(barrier, inc=1, device_id=partner, device_id_type=MESH)

    row = lax.broadcasted_iota(jnp.int32, (128, 128), 0)
    lane = lax.broadcasted_iota(jnp.int32, (128, 128), 1)
    ids = ids_ref[...]
    probs = probs_ref[...]
    expert_of = (row >> 1) & 7
    hosted = jnp.zeros((128, 128), jnp.int32)
    for w in range(8):
        hosted = jnp.where(expert_of == w, hosted_ref[w], hosted)
    matched = jnp.zeros((128, 128), F32)
    prob_at = jnp.zeros((128, 128), F32)
    for k in range(8):
        hit = (ids[k : k + 1, :] == hosted).astype(F32)
        matched = matched + hit
        prob_at = prob_at + hit * probs[k : k + 1, :]
    before = (row < lane).astype(BF)
    rank = jnp.dot(matched.astype(BF), before, preferred_element_type=F32)
    cap_of = ((row >> 4) & 1) * 2 + (row & 1)
    chosen = matched * (rank == cap_of.astype(F32)).astype(F32)
    table = prob_at * chosen
    select = chosen[:32].astype(BF)
    slot_prob = jnp.sum(table[:32], axis=1, keepdims=True)
    select_ref[...] = select

    def moved(q):
        return ((q >> 1) & 7) * 16 + (q >> 5) * 4 + ((q >> 4) & 1) * 2 + (q & 1)

    perm[...] = (lane == moved(row)).astype(BF)
    permt[...] = (row == moved(lane)).astype(BF)

    def x_copy(arr, q, k, back):
        xd, cd = lax.rem(x + lax.div(k, 2), 4), lax.rem(c + lax.rem(k, 2), 2)
        there = xd * 2 + cd
        if back:
            return rcopy(xback.at[arr, q, there], eo.at[arr, me_dp, pl.ds(q * 16, 16)], xb_s.at[arr, q], xb_r.at[arr, q], dev(xd, cd, y, z))
        return rcopy(xsend.at[arr, q, there], xbuf.at[arr, q, me_dp], xs_s.at[arr, q], xs_r.at[arr, q], dev(xd, cd, y, z))

    def x_send(arr, q, back):
        def body(i, carry):
            x_copy(arr, q, lax.rem(i + 3, 7) + 1, back).start()
            return carry

        lax.fori_loop(0, 7, body, 0)

    def x_wait(arr, q, back):
        wait_in(eo.at[arr, pl.ds(0, 7), pl.ds(q * 16, 16)] if back else xbuf.at[arr, q, pl.ds(0, 7)], (xb_r if back else xs_r).at[arr, q])

    def wait_out(src, ssem):
        rcopy(src, src, ssem, ssem, other_core).wait_send()

    def gather_rows(arr):
        def body(index, carry):
            columns = pl.ds(pl.multiple_of(index * width, 128), width)
            source = tokens if arr == 0 else ograd
            rows = jnp.dot(select, source[:, columns], preferred_element_type=F32)
            if arr == 1:
                rows = slot_prob * rows
            rows = rows.astype(BF)
            for q in (0, 1):
                xsend[arr, q, index] = rows[q * 16 : q * 16 + 16]
            return carry

        lax.fori_loop(0, 8, body, 0)
        for q in (0, 1):
            xbuf[arr, q, me_dp] = xsend[arr, q, me_dp]

    def y_copy(arr, q, k, back):
        yd = lax.rem(y + k, 4)
        if back:
            src = zout.at[arr, q, :, pl.ds(pl.multiple_of(yd * 16, 16), 16)]
            return rcopy(src, yback.at[arr, q, y], yb_s.at[arr, q], yb_r.at[arr, q], dev(x, c, yd, z))
        dst = zsrc.at[arr, q, :, pl.ds(pl.multiple_of(y * 16, 16), 16)]
        return rcopy(ysend.at[arr, q, yd], dst, ys_s.at[arr, q], ys_r.at[arr, q], dev(x, c, yd, z))

    def y_stage(arr, q):
        x_wait(arr, q, False)
        rows = jnp.dot(perm[...], xbuf[arr, q].reshape(128, width), preferred_element_type=F32).astype(BF)
        ysend[arr, q] = rows.reshape(4, 2, 16, width)
        for k in (2, 1, 3):
            y_copy(arr, q, k, False).start()
        mine = pl.ds(pl.multiple_of(y * 16, 16), 16)
        zsrc[arr, q, :, mine] = ysend[arr, q, y]

    def y_wait(arr, q):
        wait_in(zsrc.at[arr, q, :, pl.ds(0, 48)], ys_r.at[arr, q])

    right0, left0 = lax.rem(z + 2, 8), lax.rem(13 - z, 8)

    def each_line(body):
        def line(i, carry):
            d, half = lax.div(i, 2), lax.rem(i, 2)
            body(d, half, lax.rem(right0 + d * (left0 + 8 - right0) + 4 * half, 8))
            return carry

        lax.fori_loop(0, 4, line, 0)

    def origin_z(d, s):
        return lax.rem(z + 8 - (1 - 2 * d) * s, 8)

    def z_dev(d, back):
        step = (2 * d - 1) if back else (1 - 2 * d)
        return dev(x, c, y, lax.rem(z + 8 + step, 8))

    def is_zero(p):
        return lax.div(7 - p, 7)

    def is_one(p):
        return is_zero(lax.rem(p + 7, 8))

    def z_send(arr, q, d, half, p, s):
        src = origin_z(d, s)
        if s == 0:
            first = is_zero(p)
            slot = src + first * (8 + d - src)
            rcopy(zsrc.at[arr, q, half], tokin.at[arr, q, slot], zs_s.at[arr, q, d, half], zs_r.at[arr, q, d, 1 - first], z_dev(d, False)).start()
        else:
            came = src + is_one(p) * (8 + d - src) if s == 1 else src
            rcopy(tokin.at[arr, q, came], tokin.at[arr, q, src], zs_s.at[arr, q, d, half], zs_r.at[arr, q, d, s + 1], z_dev(d, False)).start()

    def z_sent(arr, q):
        def body(d, half, p):
            for last in range(5):

                @pl.when(p == last)
                def _():
                    wait_out(tokin.at[arr, q, pl.ds(0, last + 1)], zs_s.at[arr, q, d, half])

        each_line(body)

    def z_step(arr, q, s):
        def body(d, half, p):
            @pl.when((p >= s) & (p <= 5))
            def _():
                src = origin_z(d, s)
                transit = is_one(p) if s == 1 else 0
                wait_in(tokin.at[arr, q, src + transit * (8 + d - src)], zs_r.at[arr, q, d, s * (1 - transit)])
                if s < 5:

                    @pl.when(p <= 4)
                    def _():
                        z_send(arr, q, d, half, p, s)

        each_line(body)

    def z_begin(arr, q):
        y_wait(arr, q)
        for far in (True, False):

            def body(d, half, p):
                @pl.when(p < 4 if far else p == 4)
                def _():
                    z_send(arr, q, d, half, p, 0)

            each_line(body)
        tokin[arr, q, z] = zsrc[arr, q, myhalf]

    def forward(arr, q):
        def body(i, carry):
            rows = tokin[arr, q, pl.ds(4 * i, 4)].reshape(256, width)
            two = pl.ds(2 * i, 2)
            if arr == 0:
                part[0, q, two] = jnp.dot(rows, wg[...], preferred_element_type=F32).reshape(2, 2, 64, 512)
                part[1, q, two] = jnp.dot(rows, wu[...], preferred_element_type=F32).reshape(2, 2, 64, 512)
            else:
                part[2, q, two] = lax.dot_general(rows, wd[...], NT, preferred_element_type=F32).reshape(2, 2, 64, 512)
            return carry

        lax.fori_loop(0, 2, body, 0)
        c_copy(arr, q).start()

    kinds = (pl.ds(0, 2), pl.ds(2, 1))
    which = ((0, 1), (2,))

    def c_copy(g, q):
        return rcopy(part.at[kinds[g], q, :, 1 - c], rs.at[kinds[g], q], cx_s.at[g, q], cx_r.at[g, q], other_core)

    low, high = pl.ds(0, 256), pl.ds(256, 256)
    ahead, behind, across = lax.rem(x + 1, 4), lax.rem(x + 3, 4), lax.rem(x + 2, 4)

    def rx_copies(g, q):
        ks = kinds[g]
        return [
            rcopy(src, dst, rx_s.at[g, q], rx_r.at[g, q, min(k, 2)], to)
            for k, (src, dst, to) in enumerate((
                (rs.at[ks, q, across, :, low], xr1.at[R, ks, q], xr_dev),
                (rs.at[ks, q, across, :, high], xr1.at[L, ks, q], xl_dev),
                (rs.at[ks, q, ahead, :, high], fin.at[0, ks, q], xr_dev),
                (rs.at[ks, q, behind, :, low], fin.at[1, ks, q], xl_dev),
                (xr1.at[R, ks, q], fin.at[2, ks, q], xr_dev),
                (xr1.at[L, ks, q], fin.at[3, ks, q], xl_dev),
            ))
        ]

    def rs_one(g, q):
        c_copy(g, q).wait_recv()
        copies = rx_copies(g, q)

        def add(chunk):
            for j in which[g]:
                rs[j, q, chunk] = part[j, q, chunk, c] + rs[j, q, chunk]

        add(across)
        copies[0].start()
        copies[1].start()
        add(ahead)
        copies[2].start()
        add(behind)
        copies[3].start()
        add(x)

    def rs_two(g, q):
        copies = rx_copies(g, q)
        copies[0].wait_recv()
        for j in which[g]:
            xr1[R, j, q] = xr1[R, j, q] + rs[j, q, ahead, :, low]
        copies[4].start()
        copies[1].wait_recv()
        for j in which[g]:
            xr1[L, j, q] = xr1[L, j, q] + rs[j, q, behind, :, high]
        copies[5].start()

    def rs_end(g, q):
        wait_in(fin.at[:, kinds[g], q], rx_r.at[g, q, 2])
        for j in which[g]:
            own[j, q, :, low] = rs[j, q, x, :, low] + fin[1, j, q] + fin[2, j, q]
            own[j, q, :, high] = rs[j, q, x, :, high] + fin[0, j, q] + fin[3, j, q]
        gate = own[0, q]
        up = own[1, q]
        sig = jax.nn.sigmoid(gate)
        silu = gate * sig
        if g == 0:
            acts[0, q, me_dp] = (silu * up).astype(BF)
        else:
            back = own[2, q]
            acts[1, q, me_dp] = (back * up * sig * (1.0 + gate * (1.0 - sig))).astype(BF)
            acts[2, q, me_dp] = (back * silu).astype(BF)
        for k in range(3):
            ag_copy(g, q, k).start()

    held = (pl.ds(0, 1), pl.ds(1, 2))

    def ag_copy(g, q, k):
        ks = held[g]
        before_me, after_me, far = behind * 2 + c, ahead * 2 + c, across * 2 + c
        what, where = (
            (acts.at[ks, q, me_dp], xr_dev),
            (acts.at[ks, q, me_dp], xl_dev),
            (acts.at[ks, q, me_dp], other_core),
            (acts.at[ks, q, before_me, :, low], xr_dev),
            (acts.at[ks, q, after_me, :, high], xl_dev),
            (acts.at[ks, q, before_me], other_core),
            (acts.at[ks, q, after_me], other_core),
            (acts.at[ks, q, far], other_core),
        )[k]
        return rcopy(what, what, ag_s.at[g, q], ag_r.at[g, q, (0, 1, 3, 2, 2, 3, 3, 3)[k]], where)

    def ag_wait(g, q, k):
        ks = held[g]
        dst = (
            acts.at[ks, q, behind * 2 + c],
            acts.at[ks, q, ahead * 2 + c],
            acts.at[ks, q, across * 2 + c],
            acts.at[ks, q, pl.ds(0, 4)],
        )[k]
        wait_in(dst, ag_r.at[g, q, k])

    def ag_two(g, q):
        ag_wait(g, q, 0)
        ag_copy(g, q, 3).start()
        ag_copy(g, q, 5).start()
        ag_wait(g, q, 1)
        ag_copy(g, q, 4).start()
        ag_copy(g, q, 6).start()

    def ag_three(g, q):
        ag_wait(g, q, 2)
        ag_copy(g, q, 7).start()
        ag_wait(g, q, 3)

    def partial_out(arr, q):
        def body(i, carry):
            four = pl.ds(4 * i, 4)
            if arr == 0:
                piece = jnp.dot(acts[0, q, four].reshape(256, 512), wd[...], preferred_element_type=F32)
            else:
                piece = lax.dot_general(acts[1, q, four].reshape(256, 512), wg[...], NT, preferred_element_type=F32)
                piece = piece + lax.dot_general(acts[2, q, four].reshape(256, 512), wu[...], NT, preferred_element_type=F32)
            outp[arr, q, four] = piece.astype(BF).reshape(4, 64, width)
            return carry

        lax.fori_loop(0, 2, body, 0)
        zb_begin(arr, q)

    def zb_copy(arr, q, d, half, p, s, whole):
        src = outp.at[arr, q, origin_z(d, s)] if whole else rbuf.at[arr, q, d, half, s]
        sem = s - 1
        if s == 1:
            sem = 5 * is_one(p)
        return rcopy(src, rbuf.at[arr, q, d, half, s - 1], zb_s.at[arr, q, d, half], zb_r.at[arr, q, d, sem], z_dev(d, True))

    def zb_begin(arr, q):
        def body(d, half, p):
            @pl.when(p == 5)
            def _():
                for s in (5, 4, 3, 2, 1):
                    zb_copy(arr, q, d, half, p, s, True).start()

        each_line(body)

    def zb_step(arr, q, s):
        def body(d, half, p):
            @pl.when((p >= s) & (p <= 4))
            def _():
                sem = s
                if s == 0:
                    sem = 5 * is_zero(p)
                wait_in(rbuf.at[arr, q, d, half, s], zb_r.at[arr, q, d, sem])
                if s > 0:

                    @pl.when(p >= 2)
                    def _():
                        total = rbuf[arr, q, d, half, s].astype(F32) + outp[arr, q, origin_z(d, s)].astype(F32)
                        rbuf[arr, q, d, half, s] = total.astype(BF)

                    zb_copy(arr, q, d, half, p, s, False).start()

        each_line(body)

    def zb_end(arr, q):
        zb_step(arr, q, 0)
        for half in (0, 1):
            pr, pleft = lax.rem(right0 + 4 * half, 8), lax.rem(left0 + 4 * half, 8)

            def put(*refs):
                total = refs[0][...].astype(F32)
                for ref in refs[1:]:
                    total = total + ref[...].astype(F32)
                zout[arr, q, half] = total.astype(BF)

            right, left, mine = rbuf.at[arr, q, R, half, 0], rbuf.at[arr, q, L, half, 0], outp.at[arr, q, z]

            @pl.when((myhalf == half) & (pr <= 4) & (pleft <= 4))
            def _():
                put(mine, right, left)

            @pl.when((myhalf == half) & (pr <= 4) & (pleft > 4))
            def _():
                put(mine, right)

            @pl.when((myhalf == half) & (pr > 4) & (pleft <= 4))
            def _():
                put(mine, left)

            @pl.when((myhalf != half) & (pr <= 4))
            def _():
                put(right)

            @pl.when((myhalf != half) & (pleft <= 4))
            def _():
                put(left)

        for k in (2, 1, 3):
            y_copy(arr, q, k, True).start()
        yback[arr, q, y] = zout[arr, q, :, pl.ds(pl.multiple_of(y * 16, 16), 16)]

    def zb_sent(arr, q):
        def body(d, half, p):
            for last in range(1, 6):

                @pl.when(p == last)
                def _():
                    wait_out(outp.at[arr, q, pl.ds(0, last)], zb_s.at[arr, q, d, half])

        each_line(body)

    def x_back(arr, q):
        wait_in(yback.at[arr, q, pl.ds(0, 3)], yb_r.at[arr, q])
        rows = jnp.dot(permt[...], yback[arr, q].reshape(128, width), preferred_element_type=F32).astype(BF)
        xback[arr, q] = rows.reshape(8, 16, width)
        x_send(arr, q, True)
        eo[arr, me_dp, pl.ds(q * 16, 16)] = xback[arr, q, me_dp]

    def weight_grad(kind, piece):
        def body(i, carry):
            tile = pl.ds(pl.multiple_of(i * 128, 128), 128)
            total = jnp.zeros((128, 512 if kind < 2 else width), F32)
            for q in (0, 1):
                if kind < 2:
                    lhs = tokin[0, q, pl.ds(0, 8), :, tile].reshape(512, 128)
                    rhs = acts[1 + kind, q].reshape(512, 512)
                else:
                    lhs = acts[0, q, :, :, tile].reshape(512, 128)
                    rhs = tokin[1, q, pl.ds(0, 8)].reshape(512, width)
                total = total + lax.dot_general(lhs, rhs, TN, preferred_element_type=F32)
            (ggrad, ugrad, dgrad)[kind][tile, :] = total.astype(BF)
            return carry

        tiles = width // 128 if kind < 2 else 4
        lax.fori_loop(piece * tiles // 3, (piece + 1) * tiles // 3, body, 0)
        if piece == 2:
            stores[1 + kind].start()

    def token_side():
        x_wait(0, 0, True)
        x_wait(0, 1, True)
        big = table.astype(BF).astype(F32)
        rest = table - big
        mid = rest.astype(BF).astype(F32)
        small = (rest - mid).astype(BF).astype(F32)
        split = jnp.where(row < 32, big, jnp.where(row < 64, mid, jnp.where(row < 96, small, 0.0))).T.astype(BF)

        def body(share, scores):
            columns = pl.ds(pl.multiple_of(share * width, 128), width)
            outs = eo[0, share]
            mixed[:, columns] = jnp.dot(split, jnp.concatenate([outs] * 4, axis=0), preferred_element_type=F32).astype(BF)
            return scores + lax.dot_general(outs, ograd[:, columns], NT, preferred_element_type=F32)

        scores = lax.fori_loop(0, 8, body, jnp.zeros((32, 128), F32))
        stores[0].start()
        weighted = chosen[:32] * scores
        for k in range(8):
            hit = (ids[k : k + 1, :] == hosted[:32]).astype(F32)
            pgrad_ref[k : k + 1, :] = jnp.sum(hit * weighted, axis=0, keepdims=True)

    def sent_mid(g, q):
        c_copy(g, q).wait_send()
        wait_out(rs.at[kinds[g], q, pl.ds(0, 3)], rx_s.at[g, q])
        wait_out(acts.at[held[g], q, pl.ds(0, 7)], ag_s.at[g, q])

    def sent_in(arr, q):
        wait_out(xsend.at[arr, q, pl.ds(0, 7)], xs_s.at[arr, q])
        wait_out(ysend.at[arr, q, pl.ds(0, 3)], ys_s.at[arr, q])
        z_sent(arr, q)

    def sent_out(arr, q):
        zb_sent(arr, q)
        wait_out(zout.at[arr, q, :, pl.ds(0, 48)], yb_s.at[arr, q])
        wait_out(xback.at[arr, q, pl.ds(0, 7)], xb_s.at[arr, q])

    T, G = 0, 1
    loads[0].wait()
    gather_rows(T)
    pl.semaphore_wait(barrier, len(partners))
    x_send(T, 0, False)
    x_send(T, 1, False)
    loads[1].wait()
    gather_rows(G)
    y_stage(T, 0)
    x_send(G, 0, False)
    x_send(G, 1, False)
    y_stage(T, 1)
    z_begin(T, 0)
    z_step(T, 0, 1)
    z_begin(T, 1)
    y_stage(G, 0)
    z_step(T, 0, 2)
    z_step(T, 1, 1)
    z_step(T, 0, 3)
    z_step(T, 0, 4)
    z_step(T, 1, 2)
    z_begin(G, 0)
    z_step(T, 0, 5)
    for load in loads[2:]:
        load.wait()
    forward(T, 0)
    z_step(T, 1, 3)
    rs_one(T, 0)
    y_stage(G, 1)
    z_step(T, 1, 4)
    z_step(G, 0, 1)
    rs_two(T, 0)
    z_begin(G, 1)
    z_step(T, 1, 5)
    forward(T, 1)
    rs_end(T, 0)
    z_step(G, 0, 2)
    rs_one(T, 1)
    z_step(G, 1, 1)
    ag_two(T, 0)
    rs_two(T, 1)
    z_step(G, 0, 3)
    z_step(G, 1, 2)
    ag_three(T, 0)
    partial_out(T, 0)
    z_step(G, 0, 4)
    rs_end(T, 1)
    z_step(G, 0, 5)
    forward(G, 0)
    ag_two(T, 1)
    z_step(G, 1, 3)
    rs_one(G, 0)
    ag_three(T, 1)
    rs_two(G, 0)
    z_step(G, 1, 4)
    partial_out(T, 1)
    z_step(G, 1, 5)
    rs_end(G, 0)
    forward(G, 1)
    ag_two(G, 0)
    weight_grad(2, 0)
    zb_step(T, 0, 4)
    zb_step(T, 1, 4)
    rs_one(G, 1)
    ag_three(G, 0)
    rs_two(G, 1)
    partial_out(G, 0)
    zb_step(T, 0, 3)
    zb_step(T, 1, 3)
    rs_end(G, 1)
    zb_step(T, 0, 2)
    zb_step(G, 0, 4)
    weight_grad(2, 1)
    zb_step(T, 1, 2)
    ag_two(G, 1)
    zb_step(G, 0, 3)
    zb_step(T, 0, 1)
    ag_three(G, 1)
    partial_out(G, 1)
    zb_step(T, 1, 1)
    weight_grad(1, 0)
    zb_end(T, 0)
    zb_step(G, 1, 4)
    weight_grad(0, 0)
    zb_step(G, 0, 2)
    zb_step(G, 1, 3)
    weight_grad(2, 2)
    zb_step(G, 0, 1)
    weight_grad(0, 1)
    zb_step(G, 1, 2)
    x_back(T, 0)
    zb_end(T, 1)
    weight_grad(0, 2)
    zb_step(G, 1, 1)
    zb_end(G, 0)
    weight_grad(1, 1)
    weight_grad(1, 2)
    x_back(T, 1)
    zb_end(G, 1)
    x_back(G, 0)
    x_back(G, 1)
    token_side()
    for arr in (T, G):
        for q in (0, 1):
            sent_in(arr, q)
            sent_mid(arr, q)
    for arr, q in ((T, 0), (T, 1), (G, 0)):
        sent_out(arr, q)
    x_wait(G, 0, True)
    x_wait(G, 1, True)
    stores[4].start()
    sent_out(G, 1)
    for store in stores:
        store.wait()


def finish(width, mixed_in, ggrad_in, ugrad_in, dgrad_in, back, select, pgrad_in, mixed, igrad, pgrad, ggrad, ugrad, dgrad, held, gbuf, ubuf, dbuf, tile, isem, osem, tsem):
    moves = []
    for i in range(4):
        rows = pl.ds(i * 32, 32)
        moves.append((mixed_in.at[rows], held.at[rows], mixed.at[rows]))
    moves += [(ggrad_in, gbuf, ggrad), (ugrad_in, ubuf, ugrad), (dgrad_in, dbuf, dgrad)]
    come = [pltpu.make_async_copy(a, b, isem.at[i]) for i, (a, b, _) in enumerate(moves)]
    leave = [pltpu.make_async_copy(b, o, osem.at[i]) for i, (_, b, o) in enumerate(moves)]
    for move in come:
        move.start()
    pgrad[...] = pgrad_in[...]
    outs = []
    for share in range(8):
        columns = pl.ds(share * width, width)
        tile[:, columns] = lax.dot_general(select[...], back[share], TN, preferred_element_type=F32).astype(BF)
        outs.append(pltpu.make_async_copy(tile.at[:, columns], igrad.at[:, columns], tsem.at[share]))
        outs[-1].start()
        if share < 7:
            come[share].wait()
            leave[share].start()
    for out in outs + leave:
        out.wait()


def on_device(tokens, out_grad, expert_ids, route_probs, hosted, gate_weight, up_weight, down_weight):
    model_width = tokens.shape[1]
    width, hidden = gate_weight.shape
    vmem = pl.BlockSpec(memory_space=pltpu.VMEM)
    smem = pl.BlockSpec(memory_space=pltpu.SMEM)
    hbm = pl.BlockSpec(memory_space=pl.ANY)
    dma = pltpu.SemaphoreType.DMA
    row_shape = jax.ShapeDtypeStruct(tokens.shape, BF)
    side_shape = jax.ShapeDtypeStruct((8, 128), F32)
    grads = (
        jax.ShapeDtypeStruct(gate_weight.shape, BF),
        jax.ShapeDtypeStruct(up_weight.shape, BF),
        jax.ShapeDtypeStruct(down_weight.shape, BF),
    )
    mixed, pgrad, ggrad, ugrad, dgrad, back, select = pl.pallas_call(
        functools.partial(kernel, width),
        out_shape=(
            row_shape, side_shape, *grads,
            jax.ShapeDtypeStruct((8, 32, width), BF),
            jax.ShapeDtypeStruct((32, 128), BF),
        ),
        in_specs=[vmem, vmem, smem] + [hbm] * 5,
        out_specs=(hbm, vmem, hbm, hbm, hbm, hbm, vmem),
        scratch_shapes=[
            pltpu.VMEM((128, model_width), BF),
            pltpu.VMEM((128, model_width), BF),
            pltpu.VMEM((width, hidden), BF),
            pltpu.VMEM((width, hidden), BF),
            pltpu.VMEM((hidden, width), BF),
            pltpu.VMEM((128, model_width), BF),
            pltpu.VMEM((width, hidden), BF),
            pltpu.VMEM((width, hidden), BF),
            pltpu.VMEM((hidden, width), BF),
            pltpu.VMEM((2, 2, 8, 16, width), BF),
            pltpu.VMEM((2, 2, 8, 16, width), BF),
            pltpu.VMEM((2, 2, 4, 2, 16, width), BF),
            pltpu.VMEM((2, 2, 2, 64, width), BF),
            pltpu.VMEM((2, 2, 10, 64, width), BF),
            pltpu.VMEM((3, 2, 4, 2, 64, hidden), F32),
            pltpu.VMEM((3, 2, 4, 64, hidden), F32),
            pltpu.VMEM((2, 3, 2, 64, hidden // 2), F32),
            pltpu.VMEM((4, 3, 2, 64, hidden // 2), F32),
            pltpu.VMEM((3, 2, 64, hidden), F32),
            pltpu.VMEM((3, 2, 8, 64, hidden), BF),
            pltpu.VMEM((2, 2, 8, 64, width), BF),
            pltpu.VMEM((2, 2, 2, 2, 5, 64, width), BF),
            pltpu.VMEM((2, 2, 2, 64, width), BF),
            pltpu.VMEM((2, 2, 4, 2, 16, width), BF),
            pltpu.VMEM((2, 2, 8, 16, width), BF),
            pltpu.VMEM((2, 8, 32, width), BF),
            pltpu.VMEM((128, 128), BF),
            pltpu.VMEM((128, 128), BF),
            dma((5,)), dma((5,)),
            dma((2, 2)), dma((2, 2)), dma((2, 2)), dma((2, 2)),
            dma((2, 2, 2, 2)), dma((2, 2, 2, 6)),
            dma((2, 2)), dma((2, 2)), dma((2, 2)), dma((2, 2, 3)), dma((2, 2)), dma((2, 2, 4)),
            dma((2, 2, 2, 2)), dma((2, 2, 2, 6)), dma((2, 2)), dma((2, 2)), dma((2, 2)), dma((2, 2)),
        ],
        compiler_params=pltpu.CompilerParams(
            collective_id=0, has_side_effects=True, vmem_limit_bytes=60 * 1024 * 1024
        ),
        cost_estimate=pl.CostEstimate(flops=9 * 2 * 1024 * 896 * 512, bytes_accessed=16_000_000, transcendentals=65536),
    )(expert_ids.T, route_probs.T, hosted, tokens, out_grad, gate_weight, up_weight, down_weight)
    mixed, igrad, pgrad, ggrad, ugrad, dgrad = pl.pallas_call(
        functools.partial(finish, width),
        out_shape=(row_shape, row_shape, side_shape, *grads),
        in_specs=[hbm] * 4 + [vmem] * 3,
        out_specs=(hbm, hbm, vmem, hbm, hbm, hbm),
        scratch_shapes=[
            pltpu.VMEM((128, model_width), BF),
            pltpu.VMEM((width, hidden), BF),
            pltpu.VMEM((width, hidden), BF),
            pltpu.VMEM((hidden, width), BF),
            pltpu.VMEM((128, model_width), BF),
            dma((7,)), dma((7,)), dma((8,)),
        ],
        compiler_params=pltpu.CompilerParams(vmem_limit_bytes=60 * 1024 * 1024),
    )(mixed, ggrad, ugrad, dgrad, back, select, pgrad)
    return mixed, igrad, pgrad.T, ggrad, ugrad, dgrad


def solution(mesh):
    return jax.shard_map(
        on_device,
        mesh=mesh,
        in_specs=(
            P(("dp", "expert"), None),
            P(("dp", "expert"), None),
            P(("dp", "expert"), None),
            P(("dp", "expert"), None),
            P(),
            P("dp", "expert"),
            P("dp", "expert"),
            P("expert", "dp"),
        ),
        out_specs=(
            P(("dp", "expert"), None),
            P(("dp", "expert"), None),
            P(("dp", "expert"), None),
            P("dp", "expert"),
            P("dp", "expert"),
            P("expert", "dp"),
        ),
        check_vma=False,
    )
```

```python
import functools

import jax
import jax.numpy as jnp
from jax import lax
from jax.experimental import pallas as pl
from jax.experimental.pallas import tpu as pltpu
from jax.sharding import PartitionSpec as P

BF = jnp.bfloat16
F32 = jnp.float32
MESH = pl.DeviceIdType.MESH
NT = (((1,), (1,)), ((), ()))
TN = (((0,), (0,)), ((), ()))
R, L = 0, 1


def kernel(
    width,
    ids_ref, probs_ref, hosted_ref, tokens_hbm, ograd_hbm, wg_hbm, wu_hbm, wd_hbm,
    split_ref, pgrad_ref, ggrad_hbm, ugrad_hbm, dgrad_hbm, eo_hbm, select_ref,
    tokens, ograd, wg, wu, wd, ggrad, ugrad, dgrad,
    xsend, xbuf, ysend, zsrc, tokin,
    part, rs, xr1, fin, own, acts,
    outp, rbuf, zout, yback, xback, eo, perm, permt,
    insem, outsem, xs_s, xs_r, ys_s, ys_r, zs_s, zs_r,
    cx_s, cx_r, rx_s, rx_r, ag_s, ag_r,
    zb_s, zb_r, yb_s, yb_r, xb_s, xb_r,
):
    me_dp = lax.axis_index("dp")
    me_e = lax.axis_index("expert")
    x, c = lax.div(me_dp, 2), lax.rem(me_dp, 2)
    y, z = lax.div(me_e, 8), lax.rem(me_e, 8)
    myhalf = lax.div(z, 4)

    def dev(x_, c_, y_, z_):
        return (x_ * 2 + c_, y_ * 8 + z_)

    def rcopy(src, dst, ssem, rsem, where):
        return pltpu.make_async_remote_copy(
            src_ref=src, dst_ref=dst, send_sem=ssem, recv_sem=rsem,
            device_id=where, device_id_type=MESH,
        )

    other_core = dev(x, 1 - c, y, z)
    xr_dev = dev(lax.rem(x + 1, 4), c, y, z)
    xl_dev = dev(lax.rem(x + 3, 4), c, y, z)

    def wait_in(dst, rsem):
        rcopy(dst, dst, rsem, rsem, other_core).wait_recv()

    loads = [
        pltpu.make_async_copy(a, b, insem.at[i])
        for i, (a, b) in enumerate(
            ((tokens_hbm, tokens), (ograd_hbm, ograd), (wg_hbm, wg), (wu_hbm, wu), (wd_hbm, wd))
        )
    ]
    for load in loads:
        load.start()
    stores = [
        pltpu.make_async_copy(a, b, outsem.at[i])
        for i, (a, b) in enumerate(
            ((eo.at[0], eo_hbm.at[0]), (ggrad, ggrad_hbm), (ugrad, ugrad_hbm), (dgrad, dgrad_hbm), (eo.at[1], eo_hbm.at[1]))
        )
    ]

    barrier = pltpu.get_barrier_semaphore()
    partners = []
    for kx in range(4):
        for kc in range(2):
            if kx or kc:
                partners.append(dev(lax.rem(x + kx, 4), lax.rem(c + kc, 2), y, z))
    for k in range(1, 4):
        partners.append(dev(x, c, lax.rem(y + k, 4), z))
    partners += [dev(x, c, y, lax.rem(z + 1, 8)), dev(x, c, y, lax.rem(z + 7, 8))]
    for partner in partners:
        pl.semaphore_signal(barrier, inc=1, device_id=partner, device_id_type=MESH)

    row = lax.broadcasted_iota(jnp.int32, (128, 128), 0)
    lane = lax.broadcasted_iota(jnp.int32, (128, 128), 1)
    ids = ids_ref[...]
    probs = probs_ref[...]
    expert_of = (row >> 1) & 7
    hosted = jnp.zeros((128, 128), jnp.int32)
    for w in range(8):
        hosted = jnp.where(expert_of == w, hosted_ref[w], hosted)
    matched = jnp.zeros((128, 128), F32)
    prob_at = jnp.zeros((128, 128), F32)
    for k in range(8):
        hit = (ids[k : k + 1, :] == hosted).astype(F32)
        matched = matched + hit
        prob_at = prob_at + hit * probs[k : k + 1, :]
    before = (row < lane).astype(BF)
    rank = jnp.dot(matched.astype(BF), before, preferred_element_type=F32)
    cap_of = ((row >> 4) & 1) * 2 + (row & 1)
    chosen = matched * (rank == cap_of.astype(F32)).astype(F32)
    table = prob_at * chosen
    select = chosen[:32].astype(BF)
    slot_prob = jnp.sum(table[:32], axis=1, keepdims=True)
    select_ref[...] = select

    def moved(q):
        return ((q >> 1) & 7) * 16 + (q >> 5) * 4 + ((q >> 4) & 1) * 2 + (q & 1)

    perm[...] = (lane == moved(row)).astype(BF)
    permt[...] = (row == moved(lane)).astype(BF)

    def x_copy(arr, q, k, back):
        xd, cd = lax.rem(x + lax.div(k, 2), 4), lax.rem(c + lax.rem(k, 2), 2)
        there = xd * 2 + cd
        if back:
            return rcopy(xback.at[arr, q, there], eo.at[arr, me_dp, pl.ds(q * 16, 16)], xb_s.at[arr, q], xb_r.at[arr, q], dev(xd, cd, y, z))
        return rcopy(xsend.at[arr, q, there], xbuf.at[arr, q, me_dp], xs_s.at[arr, q], xs_r.at[arr, q], dev(xd, cd, y, z))

    def x_send(arr, q, back):
        def body(i, carry):
            x_copy(arr, q, lax.rem(i + 3, 7) + 1, back).start()
            return carry

        lax.fori_loop(0, 7, body, 0)

    def x_wait(arr, q, back):
        wait_in(eo.at[arr, pl.ds(0, 7), pl.ds(q * 16, 16)] if back else xbuf.at[arr, q, pl.ds(0, 7)], (xb_r if back else xs_r).at[arr, q])

    def wait_out(src, ssem):
        rcopy(src, src, ssem, ssem, other_core).wait_send()

    def gather_rows(arr):
        def body(index, carry):
            columns = pl.ds(pl.multiple_of(index * width, 128), width)
            source = tokens if arr == 0 else ograd
            rows = jnp.dot(select, source[:, columns], preferred_element_type=F32)
            if arr == 1:
                rows = slot_prob * rows
            rows = rows.astype(BF)
            for q in (0, 1):
                xsend[arr, q, index] = rows[q * 16 : q * 16 + 16]
            return carry

        lax.fori_loop(0, 8, body, 0)
        for q in (0, 1):
            xbuf[arr, q, me_dp] = xsend[arr, q, me_dp]

    def y_copy(arr, q, k, back):
        yd = lax.rem(y + k, 4)
        if back:
            src = zout.at[arr, q, :, pl.ds(pl.multiple_of(yd * 16, 16), 16)]
            return rcopy(src, yback.at[arr, q, y], yb_s.at[arr, q], yb_r.at[arr, q], dev(x, c, yd, z))
        dst = zsrc.at[arr, q, :, pl.ds(pl.multiple_of(y * 16, 16), 16)]
        return rcopy(ysend.at[arr, q, yd], dst, ys_s.at[arr, q], ys_r.at[arr, q], dev(x, c, yd, z))

    def y_stage(arr, q):
        x_wait(arr, q, False)
        rows = jnp.dot(perm[...], xbuf[arr, q].reshape(128, width), preferred_element_type=F32).astype(BF)
        ysend[arr, q] = rows.reshape(4, 2, 16, width)
        for k in (2, 1, 3):
            y_copy(arr, q, k, False).start()
        mine = pl.ds(pl.multiple_of(y * 16, 16), 16)
        zsrc[arr, q, :, mine] = ysend[arr, q, y]

    def y_wait(arr, q):
        wait_in(zsrc.at[arr, q, :, pl.ds(0, 48)], ys_r.at[arr, q])

    right0, left0 = lax.rem(z + 2, 8), lax.rem(13 - z, 8)

    def each_half(d, body):
        def line(half, carry):
            body(half, lax.rem((right0, left0)[d] + 4 * half, 8))
            return carry

        lax.fori_loop(0, 2, line, 0)

    def slot_of(d, s):
        return (9 + (1 - 2 * d) * s) % 8

    def z_dev(d, back):
        step = (2 * d - 1) if back else (1 - 2 * d)
        return dev(x, c, y, lax.rem(z + 8 + step, 8))

    def is_zero(p):
        return lax.div(7 - p, 7)

    def is_one(p):
        return is_zero(lax.rem(p + 7, 8))

    def z_send(arr, q, d, half, p, s):
        there = slot_of(d, s + 1)
        if s == 0:
            first = is_zero(p)
            slot = there + first * (8 + d - there)
            rcopy(zsrc.at[arr, q, half], tokin.at[arr, q, slot], zs_s.at[arr, q, d, half], zs_r.at[arr, q, d, 1 - first], z_dev(d, False)).start()
        else:
            came = slot_of(d, s)
            if s == 1:
                came = came + is_one(p) * (8 + d - came)
            rcopy(tokin.at[arr, q, came], tokin.at[arr, q, there], zs_s.at[arr, q, d, half], zs_r.at[arr, q, d, s + 1], z_dev(d, False)).start()

    def z_sent(arr, q):
        for d in (R, L):

            def body(half, p):
                for last in range(5):

                    @pl.when(p == last)
                    def _():
                        wait_out(tokin.at[arr, q, pl.ds(0, last + 1)], zs_s.at[arr, q, d, half])

            each_half(d, body)

    def z_step(arr, q, s, d):
        def body(half, p):
            @pl.when((p >= s) & (p <= 5))
            def _():
                slot = slot_of(d, s)
                transit = 0
                if s == 1:
                    transit = is_one(p)
                    slot = slot + transit * (8 + d - slot)
                wait_in(tokin.at[arr, q, slot], zs_r.at[arr, q, d, s * (1 - transit)])
                if s < 5:

                    @pl.when(p <= 4)
                    def _():
                        z_send(arr, q, d, half, p, s)

        each_half(d, body)

    def z_own(arr, q, far):
        for d in (R, L):

            def body(half, p):
                @pl.when(p < 4 if far else p == 4)
                def _():
                    z_send(arr, q, d, half, p, 0)

            each_half(d, body)

    def z_far(arr, q):
        y_wait(arr, q)
        z_own(arr, q, True)
        tokin[arr, q, 1] = zsrc[arr, q, myhalf]

    def z_near(arr, q):
        z_own(arr, q, False)

    def forward(arr, q, part_of):
        m = 2 * q + part_of
        rows = tokin[arr, q, pl.ds(4 * part_of, 4)].reshape(256, width)
        if arr == 0:
            part[0, m] = jnp.dot(rows, wg[...], preferred_element_type=F32).reshape(4, 2, 32, 512)
            part[1, m] = jnp.dot(rows, wu[...], preferred_element_type=F32).reshape(4, 2, 32, 512)
        else:
            part[2, m] = lax.dot_general(rows, wd[...], NT, preferred_element_type=F32).reshape(4, 2, 32, 512)
        c_copy(arr, m).start()

    kinds = (pl.ds(0, 2), pl.ds(2, 1))
    which = ((0, 1), (2,))

    def c_copy(g, q):
        return rcopy(part.at[kinds[g], q, :, 1 - c], rs.at[kinds[g], q], cx_s.at[g, q], cx_r.at[g, q], other_core)

    low, high = pl.ds(0, 256), pl.ds(256, 256)
    ahead, behind, across = lax.rem(x + 1, 4), lax.rem(x + 3, 4), lax.rem(x + 2, 4)

    def rx_copies(g, q):
        ks = kinds[g]
        return [
            rcopy(src, dst, rx_s.at[g, q], rx_r.at[g, q, min(k, 2)], to)
            for k, (src, dst, to) in enumerate((
                (rs.at[ks, q, across, :, low], xr1.at[R, ks, q], xr_dev),
                (rs.at[ks, q, across, :, high], xr1.at[L, ks, q], xl_dev),
                (rs.at[ks, q, ahead, :, high], fin.at[0, ks, q], xr_dev),
                (rs.at[ks, q, behind, :, low], fin.at[1, ks, q], xl_dev),
                (xr1.at[R, ks, q], fin.at[2, ks, q], xr_dev),
                (xr1.at[L, ks, q], fin.at[3, ks, q], xl_dev),
            ))
        ]

    def rs_one(g, q):
        c_copy(g, q).wait_recv()
        copies = rx_copies(g, q)

        def add(chunk):
            for j in which[g]:
                rs[j, q, chunk] = part[j, q, chunk, c] + rs[j, q, chunk]

        add(across)
        copies[0].start()
        copies[1].start()
        add(ahead)
        copies[2].start()
        add(behind)
        copies[3].start()
        add(x)

    def rs_two(g, q):
        copies = rx_copies(g, q)
        copies[0].wait_recv()
        for j in which[g]:
            xr1[R, j, q] = xr1[R, j, q] + rs[j, q, ahead, :, low]
        copies[4].start()
        copies[1].wait_recv()
        for j in which[g]:
            xr1[L, j, q] = xr1[L, j, q] + rs[j, q, behind, :, high]
        copies[5].start()

    def rs_end(g, q):
        wait_in(fin.at[:, kinds[g], q], rx_r.at[g, q, 2])
        for j in which[g]:
            own[j, q, :, low] = rs[j, q, x, :, low] + fin[1, j, q] + fin[2, j, q]
            own[j, q, :, high] = rs[j, q, x, :, high] + fin[0, j, q] + fin[3, j, q]
        gate = own[0, q]
        up = own[1, q]
        sig = jax.nn.sigmoid(gate)
        silu = gate * sig
        if g == 0:
            acts[0, q, me_dp] = (silu * up).astype(BF)
        else:
            back = own[2, q]
            acts[1, q, me_dp] = (back * up * sig * (1.0 + gate * (1.0 - sig))).astype(BF)
            acts[2, q, me_dp] = (back * silu).astype(BF)
        for k in range(3):
            ag_copy(g, q, k).start()

    held = (pl.ds(0, 1), pl.ds(1, 2))

    def ag_copy(g, q, k):
        ks = held[g]
        before_me, after_me, far = behind * 2 + c, ahead * 2 + c, across * 2 + c
        what, where = (
            (acts.at[ks, q, me_dp], xr_dev),
            (acts.at[ks, q, me_dp], xl_dev),
            (acts.at[ks, q, me_dp], other_core),
            (acts.at[ks, q, before_me, :, low], xr_dev),
            (acts.at[ks, q, after_me, :, high], xl_dev),
            (acts.at[ks, q, before_me], other_core),
            (acts.at[ks, q, after_me], other_core),
            (acts.at[ks, q, far], other_core),
        )[k]
        return rcopy(what, what, ag_s.at[g, q], ag_r.at[g, q, (0, 1, 3, 2, 2, 3, 3, 3)[k]], where)

    def ag_wait(g, q, k):
        ks = held[g]
        dst = (
            acts.at[ks, q, behind * 2 + c],
            acts.at[ks, q, ahead * 2 + c],
            acts.at[ks, q, across * 2 + c],
            acts.at[ks, q, pl.ds(0, 4)],
        )[k]
        wait_in(dst, ag_r.at[g, q, k])

    def ag_two(g, q):
        ag_wait(g, q, 0)
        ag_copy(g, q, 3).start()
        ag_copy(g, q, 5).start()
        ag_wait(g, q, 1)
        ag_copy(g, q, 4).start()
        ag_copy(g, q, 6).start()

    def ag_fwd(g, q):
        ag_wait(g, q, 2)
        ag_copy(g, q, 7).start()

    def partial_out(arr, q, part_of):
        m = 2 * q + part_of
        ag_wait(arr, m, 3)
        if arr == 0:
            piece = jnp.dot(acts[0, m].reshape(256, 512), wd[...], preferred_element_type=F32)
        else:
            piece = lax.dot_general(acts[1, m].reshape(256, 512), wg[...], NT, preferred_element_type=F32)
            piece = piece + lax.dot_general(acts[2, m].reshape(256, 512), wu[...], NT, preferred_element_type=F32)
        outp[arr, q, pl.ds(4 * part_of, 4)] = piece.astype(BF).reshape(4, 64, width)

    def zb_copy(arr, q, d, half, p, s, whole):
        src = outp.at[arr, q, slot_of(d, s)] if whole else rbuf.at[arr, q, d, half, s]
        sem = s - 1
        if s == 1:
            sem = 5 * is_one(p)
        return rcopy(src, rbuf.at[arr, q, d, half, s - 1], zb_s.at[arr, q, d, half], zb_r.at[arr, q, d, sem], z_dev(d, True))

    def zb_begin(arr, q):
        for d in (R, L):

            def body(half, p):
                @pl.when(p == 5)
                def _():
                    for s in (5, 4, 3, 2, 1):
                        zb_copy(arr, q, d, half, p, s, True).start()

            each_half(d, body)

    def zb_step(arr, q, s, d):
        def body(half, p):
            @pl.when((p >= s) & (p <= 4))
            def _():
                sem = s
                if s == 0:
                    sem = 5 * is_zero(p)
                wait_in(rbuf.at[arr, q, d, half, s], zb_r.at[arr, q, d, sem])
                if s > 0:

                    @pl.when(p >= 2)
                    def _():
                        total = rbuf[arr, q, d, half, s].astype(F32) + outp[arr, q, slot_of(d, s)].astype(F32)
                        rbuf[arr, q, d, half, s] = total.astype(BF)

                    zb_copy(arr, q, d, half, p, s, False).start()

        each_half(d, body)

    def zb_end(arr, q):
        zb_step(arr, q, 0, R)
        zb_step(arr, q, 0, L)
        for half in (0, 1):
            pr, pleft = lax.rem(right0 + 4 * half, 8), lax.rem(left0 + 4 * half, 8)

            def put(*refs):
                total = refs[0][...].astype(F32)
                for ref in refs[1:]:
                    total = total + ref[...].astype(F32)
                zout[arr, q, half] = total.astype(BF)

            right, left, mine = rbuf.at[arr, q, R, half, 0], rbuf.at[arr, q, L, half, 0], outp.at[arr, q, 1]

            @pl.when((myhalf == half) & (pr <= 4) & (pleft <= 4))
            def _():
                put(mine, right, left)

            @pl.when((myhalf == half) & (pr <= 4) & (pleft > 4))
            def _():
                put(mine, right)

            @pl.when((myhalf == half) & (pr > 4) & (pleft <= 4))
            def _():
                put(mine, left)

            @pl.when((myhalf != half) & (pr <= 4))
            def _():
                put(right)

            @pl.when((myhalf != half) & (pleft <= 4))
            def _():
                put(left)

        for k in (2, 1, 3):
            y_copy(arr, q, k, True).start()
        yback[arr, q, y] = zout[arr, q, :, pl.ds(pl.multiple_of(y * 16, 16), 16)]

    def zb_sent(arr, q):
        for d in (R, L):

            def body(half, p):
                for last in range(1, 6):

                    @pl.when(p == last)
                    def _():
                        wait_out(outp.at[arr, q, pl.ds(0, last)], zb_s.at[arr, q, d, half])

            each_half(d, body)

    def x_back(arr, q):
        wait_in(yback.at[arr, q, pl.ds(0, 3)], yb_r.at[arr, q])
        rows = jnp.dot(permt[...], yback[arr, q].reshape(128, width), preferred_element_type=F32).astype(BF)
        xback[arr, q] = rows.reshape(8, 16, width)
        x_send(arr, q, True)
        eo[arr, me_dp, pl.ds(q * 16, 16)] = xback[arr, q, me_dp]

    def weight_grad(kind, piece):
        def body(i, carry):
            tile = pl.ds(pl.multiple_of(i * 128, 128), 128)
            total = jnp.zeros((128, 512 if kind < 2 else width), F32)
            for q in (0, 1):
                if kind < 2:
                    lhs = tokin[0, q, pl.ds(0, 8), :, tile].reshape(512, 128)
                    rhs = acts[1 + kind, pl.ds(2 * q, 2)].reshape(512, 512)
                else:
                    lhs = acts[0, pl.ds(2 * q, 2), :, :, tile].reshape(512, 128)
                    rhs = tokin[1, q, pl.ds(0, 8)].reshape(512, width)
                total = total + lax.dot_general(lhs, rhs, TN, preferred_element_type=F32)
            (ggrad, ugrad, dgrad)[kind][tile, :] = total.astype(BF)
            return carry

        tiles = width // 128 if kind < 2 else 4
        lax.fori_loop(piece * tiles // 3, (piece + 1) * tiles // 3, body, 0)
        if piece == 2:
            stores[1 + kind].start()

    def token_side():
        x_wait(0, 0, True)
        x_wait(0, 1, True)
        stores[0].start()
        big = table.astype(BF).astype(F32)
        rest = table - big
        mid = rest.astype(BF).astype(F32)
        small = (rest - mid).astype(BF).astype(F32)
        split_ref[...] = jnp.where(row < 32, big, jnp.where(row < 64, mid, jnp.where(row < 96, small, 0.0))).T.astype(BF)

        def body(share, scores):
            columns = pl.ds(pl.multiple_of(share * width, 128), width)
            outs = eo[0, share]
            return scores + lax.dot_general(outs, ograd[:, columns], NT, preferred_element_type=F32)

        scores = lax.fori_loop(0, 8, body, jnp.zeros((32, 128), F32))
        weighted = chosen[:32] * scores
        for k in range(8):
            hit = (ids[k : k + 1, :] == hosted[:32]).astype(F32)
            pgrad_ref[k : k + 1, :] = jnp.sum(hit * weighted, axis=0, keepdims=True)

    def sent_mid(g, q):
        c_copy(g, q).wait_send()
        wait_out(rs.at[kinds[g], q, pl.ds(0, 3)], rx_s.at[g, q])
        wait_out(acts.at[held[g], q, pl.ds(0, 7)], ag_s.at[g, q])

    def sent_in(arr, q):
        wait_out(xsend.at[arr, q, pl.ds(0, 7)], xs_s.at[arr, q])
        wait_out(ysend.at[arr, q, pl.ds(0, 3)], ys_s.at[arr, q])
        z_sent(arr, q)

    def sent_out(arr, q):
        zb_sent(arr, q)
        wait_out(zout.at[arr, q, :, pl.ds(0, 48)], yb_s.at[arr, q])
        wait_out(xback.at[arr, q, pl.ds(0, 7)], xb_s.at[arr, q])

    T, G = 0, 1
    loads[0].wait()
    gather_rows(T)
    pl.semaphore_wait(barrier, len(partners))
    x_send(T, 0, False)
    x_send(T, 1, False)
    y_stage(T, 0)
    loads[1].wait()
    gather_rows(G)
    x_send(G, 1, False)
    y_stage(T, 1)
    z_far(T, 0)
    z_near(T, 0)
    x_send(G, 0, False)
    z_step(T, 0, 1, R)
    z_step(T, 0, 1, L)
    z_far(T, 1)
    z_near(T, 1)
    z_step(T, 0, 2, R)
    y_stage(G, 0)
    z_step(T, 0, 2, L)
    for load in loads[2:]:
        load.wait()
    forward(T, 0, 0)
    z_step(T, 1, 1, R)
    z_step(T, 1, 1, L)
    z_far(G, 0)
    rs_one(T, 0)
    z_step(T, 0, 3, R)
    z_step(T, 0, 3, L)
    y_stage(G, 1)
    z_step(T, 1, 2, L)
    z_step(T, 1, 2, R)
    rs_two(T, 0)
    forward(T, 1, 0)
    z_step(T, 0, 4, L)
    z_step(T, 0, 4, R)
    z_step(T, 0, 5, R)
    z_near(G, 0)
    z_far(G, 1)
    rs_one(T, 2)
    z_step(T, 1, 3, R)
    z_step(T, 0, 5, L)
    z_step(T, 1, 3, L)
    z_near(G, 1)
    forward(T, 0, 1)
    rs_end(T, 0)
    z_step(G, 0, 1, L)
    rs_one(T, 1)
    z_step(G, 0, 1, R)
    ag_two(T, 0)
    rs_two(T, 1)
    z_step(T, 1, 4, L)
    z_step(T, 1, 4, R)
    z_step(G, 1, 1, L)
    z_step(G, 1, 1, R)
    rs_two(T, 2)
    rs_end(T, 1)
    z_step(G, 0, 2, R)
    z_step(G, 0, 2, L)
    ag_fwd(T, 0)
    forward(G, 0, 0)
    z_step(T, 1, 5, L)
    z_step(T, 1, 5, R)
    forward(T, 1, 1)
    ag_two(T, 1)
    partial_out(T, 0, 0)
    rs_end(T, 2)
    z_step(G, 1, 2, R)
    rs_one(G, 0)
    z_step(G, 1, 2, L)
    ag_fwd(T, 1)
    rs_one(T, 3)
    z_step(G, 0, 3, R)
    partial_out(T, 0, 1)
    zb_begin(T, 0)
    z_step(G, 0, 3, L)
    forward(G, 1, 0)
    rs_two(T, 3)
    rs_two(G, 0)
    ag_two(T, 2)
    z_step(G, 0, 4, L)
    z_step(G, 0, 4, R)
    rs_one(G, 2)
    z_step(G, 1, 3, R)
    z_step(G, 1, 3, L)
    rs_end(T, 3)
    rs_end(G, 0)
    z_step(G, 0, 5, L)
    ag_fwd(T, 2)
    z_step(G, 0, 5, R)
    forward(G, 0, 1)
    ag_two(T, 3)
    rs_two(G, 2)
    rs_one(G, 1)
    partial_out(T, 1, 0)
    ag_fwd(T, 3)
    z_step(G, 1, 4, L)
    z_step(G, 1, 4, R)
    rs_two(G, 1)
    partial_out(T, 1, 1)
    zb_begin(T, 1)
    zb_step(T, 0, 4, R)
    ag_two(G, 0)
    rs_end(G, 1)
    zb_step(T, 0, 4, L)
    ag_fwd(G, 0)
    z_step(G, 1, 5, L)
    z_step(G, 1, 5, R)
    rs_end(G, 2)
    forward(G, 1, 1)
    ag_two(G, 1)
    zb_step(T, 1, 4, R)
    weight_grad(2, 0)
    rs_one(G, 3)
    zb_step(T, 1, 4, L)
    zb_step(T, 0, 3, R)
    ag_fwd(G, 1)
    rs_two(G, 3)
    partial_out(G, 0, 0)
    partial_out(G, 0, 1)
    zb_begin(G, 0)
    zb_step(T, 1, 3, L)
    zb_step(T, 1, 3, R)
    rs_end(G, 3)
    ag_two(G, 2)
    zb_step(T, 0, 3, L)
    ag_two(G, 3)
    zb_step(G, 0, 4, R)
    zb_step(T, 0, 2, R)
    zb_step(T, 0, 2, L)
    ag_fwd(G, 2)
    zb_step(G, 0, 4, L)
    weight_grad(2, 1)
    zb_step(T, 1, 2, R)
    ag_fwd(G, 3)
    partial_out(G, 1, 0)
    zb_step(T, 1, 2, L)
    partial_out(G, 1, 1)
    zb_begin(G, 1)
    zb_step(G, 0, 3, L)
    zb_step(G, 0, 3, R)
    zb_step(T, 0, 1, L)
    zb_step(G, 1, 4, L)
    zb_step(T, 0, 1, R)
    zb_step(G, 1, 4, R)
    zb_step(G, 0, 2, R)
    zb_step(T, 1, 1, L)
    weight_grad(0, 0)
    weight_grad(1, 0)
    zb_step(G, 1, 3, R)
    zb_step(T, 1, 1, R)
    zb_step(G, 1, 3, L)
    weight_grad(2, 2)
    weight_grad(0, 1)
    zb_step(G, 0, 2, L)
    weight_grad(1, 1)
    zb_step(G, 1, 2, R)
    zb_step(G, 0, 1, R)
    zb_step(G, 1, 2, L)
    zb_end(T, 0)
    zb_step(G, 0, 1, L)
    zb_end(T, 1)
    zb_step(G, 1, 1, R)
    zb_step(G, 1, 1, L)
    x_back(T, 0)
    zb_end(G, 0)
    x_back(T, 1)
    zb_end(G, 1)
    weight_grad(0, 2)
    x_back(G, 0)
    weight_grad(1, 2)
    x_back(G, 1)
    token_side()
    for arr in (T, G):
        for q in (0, 1):
            sent_in(arr, q)
        for m in range(4):
            sent_mid(arr, m)
    for arr, q in ((T, 0), (T, 1), (G, 0)):
        sent_out(arr, q)
    x_wait(G, 0, True)
    x_wait(G, 1, True)
    stores[4].start()
    sent_out(G, 1)
    for store in stores:
        store.wait()


def finish(width, eo_in, ggrad_in, ugrad_in, dgrad_in, split, select, pgrad_in, mixed, igrad, pgrad, ggrad, ugrad, dgrad, eo, gbuf, ubuf, dbuf, mtile, itile, esem, isem, osem, tsem):
    rows = [pltpu.make_async_copy(eo_in.at[a, pl.ds(4 * h, 4)], eo.at[a, pl.ds(4 * h, 4)], esem.at[a, h]) for h in (0, 1) for a in (0, 1)]
    moves = ((ggrad_in, gbuf, ggrad), (ugrad_in, ubuf, ugrad), (dgrad_in, dbuf, dgrad))
    come = [pltpu.make_async_copy(a, b, isem.at[i]) for i, (a, b, _) in enumerate(moves)]
    leave = [pltpu.make_async_copy(b, o, osem.at[i]) for i, (_, b, o) in enumerate(moves)]
    for move in rows + come:
        move.start()
    pgrad[...] = pgrad_in[...]
    outs = []
    for pair in range(4):
        if pair % 2 == 0:
            rows[pair].wait()
            rows[pair + 1].wait()
        else:
            for k in ((0,), (1, 2))[pair // 2]:
                come[k].wait()
                leave[k].start()
        for share in (2 * pair, 2 * pair + 1):
            columns = pl.ds(share * width, width)
            mtile[:, columns] = jnp.dot(split[...], jnp.concatenate([eo[0, share]] * 4, axis=0), preferred_element_type=F32).astype(BF)
            itile[:, columns] = lax.dot_general(select[...], eo[1, share], TN, preferred_element_type=F32).astype(BF)
        columns = pl.ds(2 * pair * width, 2 * width)
        for k, (tile, to) in enumerate(((mtile, mixed), (itile, igrad))):
            outs.append(pltpu.make_async_copy(tile.at[:, columns], to.at[:, columns], tsem.at[k, pair]))
            outs[-1].start()
    for out in outs + leave:
        out.wait()


def on_device(tokens, out_grad, expert_ids, route_probs, hosted, gate_weight, up_weight, down_weight):
    model_width = tokens.shape[1]
    width, hidden = gate_weight.shape
    vmem = pl.BlockSpec(memory_space=pltpu.VMEM)
    smem = pl.BlockSpec(memory_space=pltpu.SMEM)
    hbm = pl.BlockSpec(memory_space=pl.ANY)
    dma = pltpu.SemaphoreType.DMA
    row_shape = jax.ShapeDtypeStruct(tokens.shape, BF)
    side_shape = jax.ShapeDtypeStruct((8, 128), F32)
    grads = (
        jax.ShapeDtypeStruct(gate_weight.shape, BF),
        jax.ShapeDtypeStruct(up_weight.shape, BF),
        jax.ShapeDtypeStruct(down_weight.shape, BF),
    )
    split, pgrad, ggrad, ugrad, dgrad, eo, select = pl.pallas_call(
        functools.partial(kernel, width),
        out_shape=(
            jax.ShapeDtypeStruct((128, 128), BF), side_shape, *grads,
            jax.ShapeDtypeStruct((2, 8, 32, width), BF),
            jax.ShapeDtypeStruct((32, 128), BF),
        ),
        in_specs=[vmem, vmem, smem] + [hbm] * 5,
        out_specs=(vmem, vmem, hbm, hbm, hbm, hbm, vmem),
        scratch_shapes=[
            pltpu.VMEM((128, model_width), BF),
            pltpu.VMEM((128, model_width), BF),
            pltpu.VMEM((width, hidden), BF),
            pltpu.VMEM((width, hidden), BF),
            pltpu.VMEM((hidden, width), BF),
            pltpu.VMEM((width, hidden), BF),
            pltpu.VMEM((width, hidden), BF),
            pltpu.VMEM((hidden, width), BF),
            pltpu.VMEM((2, 2, 8, 16, width), BF),
            pltpu.VMEM((2, 2, 8, 16, width), BF),
            pltpu.VMEM((2, 2, 4, 2, 16, width), BF),
            pltpu.VMEM((2, 2, 2, 64, width), BF),
            pltpu.VMEM((2, 2, 10, 64, width), BF),
            pltpu.VMEM((3, 4, 4, 2, 32, hidden), F32),
            pltpu.VMEM((3, 4, 4, 32, hidden), F32),
            pltpu.VMEM((2, 3, 4, 32, hidden // 2), F32),
            pltpu.VMEM((4, 3, 4, 32, hidden // 2), F32),
            pltpu.VMEM((3, 4, 32, hidden), F32),
            pltpu.VMEM((3, 4, 8, 32, hidden), BF),
            pltpu.VMEM((2, 2, 8, 64, width), BF),
            pltpu.VMEM((2, 2, 2, 2, 5, 64, width), BF),
            pltpu.VMEM((2, 2, 2, 64, width), BF),
            pltpu.VMEM((2, 2, 4, 2, 16, width), BF),
            pltpu.VMEM((2, 2, 8, 16, width), BF),
            pltpu.VMEM((2, 8, 32, width), BF),
            pltpu.VMEM((128, 128), BF),
            pltpu.VMEM((128, 128), BF),
            dma((5,)), dma((5,)),
            dma((2, 2)), dma((2, 2)), dma((2, 2)), dma((2, 2)),
            dma((2, 2, 2, 2)), dma((2, 2, 2, 6)),
            dma((2, 4)), dma((2, 4)), dma((2, 4)), dma((2, 4, 3)), dma((2, 4)), dma((2, 4, 4)),
            dma((2, 2, 2, 2)), dma((2, 2, 2, 6)), dma((2, 2)), dma((2, 2)), dma((2, 2)), dma((2, 2)),
        ],
        compiler_params=pltpu.CompilerParams(
            collective_id=0, has_side_effects=True, vmem_limit_bytes=60 * 1024 * 1024
        ),
        cost_estimate=pl.CostEstimate(flops=9 * 2 * 1024 * 896 * 512, bytes_accessed=16_000_000, transcendentals=65536),
    )(expert_ids.T, route_probs.T, hosted, tokens, out_grad, gate_weight, up_weight, down_weight)
    mixed, igrad, pgrad, ggrad, ugrad, dgrad = pl.pallas_call(
        functools.partial(finish, width),
        out_shape=(row_shape, row_shape, side_shape, *grads),
        in_specs=[hbm] * 4 + [vmem] * 3,
        out_specs=(hbm, hbm, vmem, hbm, hbm, hbm),
        scratch_shapes=[
            pltpu.VMEM((2, 8, 32, width), BF),
            pltpu.VMEM((width, hidden), BF),
            pltpu.VMEM((width, hidden), BF),
            pltpu.VMEM((hidden, width), BF),
            pltpu.VMEM((128, model_width), BF),
            pltpu.VMEM((128, model_width), BF),
            dma((2, 2)), dma((3,)), dma((3,)), dma((2, 4)),
        ],
        compiler_params=pltpu.CompilerParams(vmem_limit_bytes=60 * 1024 * 1024),
    )(eo, ggrad, ugrad, dgrad, split, select, pgrad)
    return mixed, igrad, pgrad.T, ggrad, ugrad, dgrad


def solution(mesh):
    return jax.shard_map(
        on_device,
        mesh=mesh,
        in_specs=(
            P(("dp", "expert"), None),
            P(("dp", "expert"), None),
            P(("dp", "expert"), None),
            P(("dp", "expert"), None),
            P(),
            P("dp", "expert"),
            P("dp", "expert"),
            P("expert", "dp"),
        ),
        out_specs=(
            P(("dp", "expert"), None),
            P(("dp", "expert"), None),
            P(("dp", "expert"), None),
            P("dp", "expert"),
            P("dp", "expert"),
            P("expert", "dp"),
        ),
        check_vma=False,
    )
```

```python
import functools

import jax
import jax.numpy as jnp
from jax import lax
from jax.experimental import pallas as pl
from jax.experimental.pallas import tpu as pltpu
from jax.sharding import PartitionSpec as P

BF = jnp.bfloat16
F32 = jnp.float32
MESH = pl.DeviceIdType.MESH
NT = (((1,), (1,)), ((), ()))
TN = (((0,), (0,)), ((), ()))
R, L = 0, 1


def kernel(
    width,
    ids_ref, probs_ref, hosted_ref, tokens_hbm, ograd_hbm, wg_hbm, wu_hbm, wd_hbm,
    split_ref, pgrad_ref, ggrad_hbm, ugrad_hbm, dgrad_hbm, eo_hbm, select_ref,
    tokens, ograd, wg, wu, wd, ggrad, ugrad, dgrad,
    xsend, xbuf, ysend, zsrc, tokin,
    part, rs, xr1, fin, own, acts,
    outp, rbuf, zout, yback, xback, eo, perm, permt,
    insem, outsem, xs_s, xs_r, ys_s, ys_r, zs_s, zs_r,
    cx_s, cx_r, rx_s, rx_r, ag_s, ag_r,
    zb_s, zb_r, yb_s, yb_r, xb_s, xb_r,
):
    me_dp = lax.axis_index("dp")
    me_e = lax.axis_index("expert")
    x, c = lax.div(me_dp, 2), lax.rem(me_dp, 2)
    y, z = lax.div(me_e, 8), lax.rem(me_e, 8)
    myhalf = lax.div(z, 4)

    def dev(x_, c_, y_, z_):
        return (x_ * 2 + c_, y_ * 8 + z_)

    def rcopy(src, dst, ssem, rsem, where):
        return pltpu.make_async_remote_copy(
            src_ref=src, dst_ref=dst, send_sem=ssem, recv_sem=rsem,
            device_id=where, device_id_type=MESH,
        )

    other_core = dev(x, 1 - c, y, z)
    xr_dev = dev(lax.rem(x + 1, 4), c, y, z)
    xl_dev = dev(lax.rem(x + 3, 4), c, y, z)

    def wait_in(dst, rsem):
        rcopy(dst, dst, rsem, rsem, other_core).wait_recv()

    loads = [
        pltpu.make_async_copy(a, b, insem.at[i])
        for i, (a, b) in enumerate(
            ((tokens_hbm, tokens), (ograd_hbm, ograd), (wg_hbm, wg), (wu_hbm, wu), (wd_hbm, wd))
        )
    ]
    for load in loads:
        load.start()
    stores = [
        pltpu.make_async_copy(a, b, outsem.at[i])
        for i, (a, b) in enumerate(
            ((eo.at[0], eo_hbm.at[0]), (ggrad, ggrad_hbm), (ugrad, ugrad_hbm), (dgrad, dgrad_hbm), (eo.at[1], eo_hbm.at[1]))
        )
    ]

    barrier = pltpu.get_barrier_semaphore()
    partners = []
    for kx in range(4):
        for kc in range(2):
            if kx or kc:
                partners.append(dev(lax.rem(x + kx, 4), lax.rem(c + kc, 2), y, z))
    for k in range(1, 4):
        partners.append(dev(x, c, lax.rem(y + k, 4), z))
    partners += [dev(x, c, y, lax.rem(z + 1, 8)), dev(x, c, y, lax.rem(z + 7, 8))]
    for partner in partners:
        pl.semaphore_signal(barrier, inc=1, device_id=partner, device_id_type=MESH)

    row = lax.broadcasted_iota(jnp.int32, (128, 128), 0)
    lane = lax.broadcasted_iota(jnp.int32, (128, 128), 1)
    ids = ids_ref[...]
    probs = probs_ref[...]
    expert_of = (row >> 1) & 7
    hosted = jnp.zeros((128, 128), jnp.int32)
    for w in range(8):
        hosted = jnp.where(expert_of == w, hosted_ref[w], hosted)
    matched = jnp.zeros((128, 128), F32)
    prob_at = jnp.zeros((128, 128), F32)
    for k in range(8):
        hit = (ids[k : k + 1, :] == hosted).astype(F32)
        matched = matched + hit
        prob_at = prob_at + hit * probs[k : k + 1, :]
    before = (row < lane).astype(BF)
    rank = jnp.dot(matched.astype(BF), before, preferred_element_type=F32)
    cap_of = ((row >> 4) & 1) * 2 + (row & 1)
    chosen = matched * (rank == cap_of.astype(F32)).astype(F32)
    table = prob_at * chosen
    select = chosen[:32].astype(BF)
    slot_prob = jnp.sum(table[:32], axis=1, keepdims=True)
    select_ref[...] = select

    def moved(q):
        return ((q >> 1) & 7) * 16 + (q >> 5) * 4 + ((q >> 4) & 1) * 2 + (q & 1)

    perm[...] = (lane == moved(row)).astype(BF)
    permt[...] = (row == moved(lane)).astype(BF)

    def x_copy(arr, q, k, back):
        xd, cd = lax.rem(x + lax.div(k, 2), 4), lax.rem(c + lax.rem(k, 2), 2)
        there = xd * 2 + cd
        if back:
            return rcopy(xback.at[arr, q, there], eo.at[arr, me_dp, pl.ds(q * 16, 16)], xb_s.at[arr, q], xb_r.at[arr, q], dev(xd, cd, y, z))
        return rcopy(xsend.at[arr, q, there], xbuf.at[arr, q, me_dp], xs_s.at[arr, q], xs_r.at[arr, q], dev(xd, cd, y, z))

    def x_send(arr, q, back):
        def body(i, carry):
            x_copy(arr, q, lax.rem(i + 3, 7) + 1, back).start()
            return carry

        lax.fori_loop(0, 7, body, 0)

    def x_wait(arr, q, back):
        wait_in(eo.at[arr, pl.ds(0, 7), pl.ds(q * 16, 16)] if back else xbuf.at[arr, q, pl.ds(0, 7)], (xb_r if back else xs_r).at[arr, q])

    def wait_out(src, ssem):
        rcopy(src, src, ssem, ssem, other_core).wait_send()

    def gather_rows(arr):
        def body(index, carry):
            columns = pl.ds(pl.multiple_of(index * width, 128), width)
            source = tokens if arr == 0 else ograd
            rows = jnp.dot(select, source[:, columns], preferred_element_type=F32)
            if arr == 1:
                rows = slot_prob * rows
            rows = rows.astype(BF)
            for q in (0, 1):
                xsend[arr, q, index] = rows[q * 16 : q * 16 + 16]
            return carry

        lax.fori_loop(0, 8, body, 0)
        for q in (0, 1):
            xbuf[arr, q, me_dp] = xsend[arr, q, me_dp]

    def y_copy(arr, q, k, back):
        yd = lax.rem(y + k, 4)
        if back:
            src = zout.at[arr, q, :, pl.ds(pl.multiple_of(yd * 16, 16), 16)]
            return rcopy(src, yback.at[arr, q, y], yb_s.at[arr, q], yb_r.at[arr, q], dev(x, c, yd, z))
        dst = zsrc.at[arr, q, :, pl.ds(pl.multiple_of(y * 16, 16), 16)]
        return rcopy(ysend.at[arr, q, yd], dst, ys_s.at[arr, q], ys_r.at[arr, q], dev(x, c, yd, z))

    def y_stage(arr, q):
        x_wait(arr, q, False)
        rows = jnp.dot(perm[...], xbuf[arr, q].reshape(128, width), preferred_element_type=F32).astype(BF)
        ysend[arr, q] = rows.reshape(4, 2, 16, width)
        for k in (2, 1, 3):
            y_copy(arr, q, k, False).start()
        mine = pl.ds(pl.multiple_of(y * 16, 16), 16)
        zsrc[arr, q, :, mine] = ysend[arr, q, y]

    def y_wait(arr, q):
        wait_in(zsrc.at[arr, q, :, pl.ds(0, 48)], ys_r.at[arr, q])

    right0, left0 = lax.rem(z + 2, 8), lax.rem(13 - z, 8)

    def each_half(d, body):
        def line(half, carry):
            body(half, lax.rem((right0, left0)[d] + 4 * half, 8))
            return carry

        lax.fori_loop(0, 2, line, 0)

    def slot_of(d, s):
        return (9 + (1 - 2 * d) * s) % 8

    def z_dev(d, back):
        step = (2 * d - 1) if back else (1 - 2 * d)
        return dev(x, c, y, lax.rem(z + 8 + step, 8))

    def is_zero(p):
        return lax.div(7 - p, 7)

    def is_one(p):
        return is_zero(lax.rem(p + 7, 8))

    def z_send(arr, q, d, half, p, s, piece):
        rows = pl.ds(32 * piece, 32)
        there = slot_of(d, s + 1)
        if s == 0:
            first = is_zero(p)
            slot = there + first * (8 + d - there)
            rcopy(zsrc.at[arr, q, half, rows], tokin.at[arr, q, slot, rows], zs_s.at[arr, q, d, half], zs_r.at[arr, q, d, 1 - first, piece], z_dev(d, False)).start()
        else:
            came = slot_of(d, s)
            if s == 1:
                came = came + is_one(p) * (8 + d - came)
            rcopy(tokin.at[arr, q, came, rows], tokin.at[arr, q, there, rows], zs_s.at[arr, q, d, half], zs_r.at[arr, q, d, s + 1, piece], z_dev(d, False)).start()

    def z_sent(arr, q):
        for d in (R, L):

            def body(half, p):
                for last in range(5):

                    @pl.when(p == last)
                    def _():
                        wait_out(tokin.at[arr, q, pl.ds(0, last + 1)], zs_s.at[arr, q, d, half])

            each_half(d, body)

    def z_step(arr, q, s, d):
        def body(half, p):
            @pl.when((p >= s) & (p <= 5))
            def _():
                slot = slot_of(d, s)
                transit = 0
                if s == 1:
                    transit = is_one(p)
                    slot = slot + transit * (8 + d - slot)
                for piece in (0, 1):
                    wait_in(tokin.at[arr, q, slot, pl.ds(32 * piece, 32)], zs_r.at[arr, q, d, s * (1 - transit), piece])
                    if s < 5:

                        @pl.when(p <= 4)
                        def _():
                            z_send(arr, q, d, half, p, s, piece)

        each_half(d, body)

    def z_own(arr, q, far):
        for d in (R, L):

            def body(half, p):
                @pl.when(p < 4 if far else p == 4)
                def _():
                    z_send(arr, q, d, half, p, 0, 0)
                    z_send(arr, q, d, half, p, 0, 1)

            each_half(d, body)

    def z_far(arr, q):
        y_wait(arr, q)
        z_own(arr, q, True)
        tokin[arr, q, 1] = zsrc[arr, q, myhalf]

    def z_near(arr, q):
        z_own(arr, q, False)

    def forward(arr, q, part_of):
        m = 2 * q + part_of
        rows = tokin[arr, q, pl.ds(4 * part_of, 4)].reshape(256, width)
        if arr == 0:
            part[0, m] = jnp.dot(rows, wg[...], preferred_element_type=F32).reshape(4, 2, 32, 512)
            part[1, m] = jnp.dot(rows, wu[...], preferred_element_type=F32).reshape(4, 2, 32, 512)
        else:
            part[2, m] = lax.dot_general(rows, wd[...], NT, preferred_element_type=F32).reshape(4, 2, 32, 512)
        c_copy(arr, m).start()

    kinds = (pl.ds(0, 2), pl.ds(2, 1))
    which = ((0, 1), (2,))

    def c_copy(g, q):
        return rcopy(part.at[kinds[g], q, :, 1 - c], rs.at[kinds[g], q], cx_s.at[g, q], cx_r.at[g, q], other_core)

    low, high = pl.ds(0, 256), pl.ds(256, 256)
    ahead, behind, across = lax.rem(x + 1, 4), lax.rem(x + 3, 4), lax.rem(x + 2, 4)

    def rx_copies(g, q):
        ks = kinds[g]
        return [
            rcopy(src, dst, rx_s.at[g, q], rx_r.at[g, q, min(k, 2)], to)
            for k, (src, dst, to) in enumerate((
                (rs.at[ks, q, across, :, low], xr1.at[R, ks, q], xr_dev),
                (rs.at[ks, q, across, :, high], xr1.at[L, ks, q], xl_dev),
                (rs.at[ks, q, ahead, :, high], fin.at[0, ks, q], xr_dev),
                (rs.at[ks, q, behind, :, low], fin.at[1, ks, q], xl_dev),
                (xr1.at[R, ks, q], fin.at[2, ks, q], xr_dev),
                (xr1.at[L, ks, q], fin.at[3, ks, q], xl_dev),
            ))
        ]

    def rs_one(g, q):
        c_copy(g, q).wait_recv()
        copies = rx_copies(g, q)

        def add(chunk):
            for j in which[g]:
                rs[j, q, chunk] = part[j, q, chunk, c] + rs[j, q, chunk]

        add(across)
        copies[0].start()
        copies[1].start()
        add(ahead)
        copies[2].start()
        add(behind)
        copies[3].start()
        add(x)

    def rs_two(g, q):
        copies = rx_copies(g, q)
        copies[0].wait_recv()
        for j in which[g]:
            xr1[R, j, q] = xr1[R, j, q] + rs[j, q, ahead, :, low]
        copies[4].start()
        copies[1].wait_recv()
        for j in which[g]:
            xr1[L, j, q] = xr1[L, j, q] + rs[j, q, behind, :, high]
        copies[5].start()

    def rs_end(g, q):
        wait_in(fin.at[:, kinds[g], q], rx_r.at[g, q, 2])
        for j in which[g]:
            own[j, q, :, low] = rs[j, q, x, :, low] + fin[1, j, q] + fin[2, j, q]
            own[j, q, :, high] = rs[j, q, x, :, high] + fin[0, j, q] + fin[3, j, q]
        gate = own[0, q]
        up = own[1, q]
        sig = jax.nn.sigmoid(gate)
        silu = gate * sig
        if g == 0:
            acts[0, q, me_dp] = (silu * up).astype(BF)
        else:
            back = own[2, q]
            acts[1, q, me_dp] = (back * up * sig * (1.0 + gate * (1.0 - sig))).astype(BF)
            acts[2, q, me_dp] = (back * silu).astype(BF)
        for k in range(3):
            ag_copy(g, q, k).start()

    held = (pl.ds(0, 1), pl.ds(1, 2))

    def ag_copy(g, q, k):
        ks = held[g]
        before_me, after_me, far = behind * 2 + c, ahead * 2 + c, across * 2 + c
        what, where = (
            (acts.at[ks, q, me_dp], xr_dev),
            (acts.at[ks, q, me_dp], xl_dev),
            (acts.at[ks, q, me_dp], other_core),
            (acts.at[ks, q, before_me, :, low], xr_dev),
            (acts.at[ks, q, after_me, :, high], xl_dev),
            (acts.at[ks, q, before_me], other_core),
            (acts.at[ks, q, after_me], other_core),
            (acts.at[ks, q, far], other_core),
        )[k]
        return rcopy(what, what, ag_s.at[g, q], ag_r.at[g, q, (0, 1, 3, 2, 2, 3, 3, 3)[k]], where)

    def ag_wait(g, q, k):
        ks = held[g]
        dst = (
            acts.at[ks, q, behind * 2 + c],
            acts.at[ks, q, ahead * 2 + c],
            acts.at[ks, q, across * 2 + c],
            acts.at[ks, q, pl.ds(0, 4)],
        )[k]
        wait_in(dst, ag_r.at[g, q, k])

    def ag_two(g, q):
        ag_wait(g, q, 0)
        ag_copy(g, q, 3).start()
        ag_copy(g, q, 5).start()
        ag_wait(g, q, 1)
        ag_copy(g, q, 4).start()
        ag_copy(g, q, 6).start()

    def ag_fwd(g, q):
        ag_wait(g, q, 2)
        ag_copy(g, q, 7).start()

    def partial_out(arr, q, part_of):
        m = 2 * q + part_of
        ag_wait(arr, m, 3)
        if arr == 0:
            piece = jnp.dot(acts[0, m].reshape(256, 512), wd[...], preferred_element_type=F32)
        else:
            piece = lax.dot_general(acts[1, m].reshape(256, 512), wg[...], NT, preferred_element_type=F32)
            piece = piece + lax.dot_general(acts[2, m].reshape(256, 512), wu[...], NT, preferred_element_type=F32)
        outp[arr, q, pl.ds(4 * part_of, 4)] = piece.astype(BF).reshape(4, 64, width)

    def zb_copy(arr, q, d, half, p, s, whole, piece):
        rows = pl.ds(32 * piece, 32)
        src = outp.at[arr, q, slot_of(d, s), rows] if whole else rbuf.at[arr, q, d, half, s, rows]
        sem = s - 1
        if s == 1:
            sem = 5 * is_one(p)
        return rcopy(src, rbuf.at[arr, q, d, half, s - 1, rows], zb_s.at[arr, q, d, half], zb_r.at[arr, q, d, sem, piece], z_dev(d, True))

    def zb_begin(arr, q):
        for d in (R, L):

            def body(half, p):
                @pl.when(p == 5)
                def _():
                    for s in (5, 4, 3, 2, 1):
                        for piece in (0, 1):
                            zb_copy(arr, q, d, half, p, s, True, piece).start()

            each_half(d, body)

    def zb_step(arr, q, s, d):
        def body(half, p):
            @pl.when((p >= s) & (p <= 4))
            def _():
                sem = s
                if s == 0:
                    sem = 5 * is_zero(p)
                for piece in (0, 1):
                    rows = pl.ds(32 * piece, 32)
                    wait_in(rbuf.at[arr, q, d, half, s, rows], zb_r.at[arr, q, d, sem, piece])
                    if s > 0:

                        @pl.when(p >= 2)
                        def _():
                            total = rbuf[arr, q, d, half, s, rows].astype(F32) + outp[arr, q, slot_of(d, s), rows].astype(F32)
                            rbuf[arr, q, d, half, s, rows] = total.astype(BF)

                        zb_copy(arr, q, d, half, p, s, False, piece).start()

        each_half(d, body)

    def zb_end(arr, q):
        zb_step(arr, q, 0, R)
        zb_step(arr, q, 0, L)
        for half in (0, 1):
            pr, pleft = lax.rem(right0 + 4 * half, 8), lax.rem(left0 + 4 * half, 8)

            def put(*refs):
                total = refs[0][...].astype(F32)
                for ref in refs[1:]:
                    total = total + ref[...].astype(F32)
                zout[arr, q, half] = total.astype(BF)

            right, left, mine = rbuf.at[arr, q, R, half, 0], rbuf.at[arr, q, L, half, 0], outp.at[arr, q, 1]

            @pl.when((myhalf == half) & (pr <= 4) & (pleft <= 4))
            def _():
                put(mine, right, left)

            @pl.when((myhalf == half) & (pr <= 4) & (pleft > 4))
            def _():
                put(mine, right)

            @pl.when((myhalf == half) & (pr > 4) & (pleft <= 4))
            def _():
                put(mine, left)

            @pl.when((myhalf != half) & (pr <= 4))
            def _():
                put(right)

            @pl.when((myhalf != half) & (pleft <= 4))
            def _():
                put(left)

        for k in (2, 1, 3):
            y_copy(arr, q, k, True).start()
        yback[arr, q, y] = zout[arr, q, :, pl.ds(pl.multiple_of(y * 16, 16), 16)]

    def zb_sent(arr, q):
        for d in (R, L):

            def body(half, p):
                for last in range(1, 6):

                    @pl.when(p == last)
                    def _():
                        wait_out(outp.at[arr, q, pl.ds(0, last)], zb_s.at[arr, q, d, half])

            each_half(d, body)

    def x_back(arr, q):
        wait_in(yback.at[arr, q, pl.ds(0, 3)], yb_r.at[arr, q])
        rows = jnp.dot(permt[...], yback[arr, q].reshape(128, width), preferred_element_type=F32).astype(BF)
        xback[arr, q] = rows.reshape(8, 16, width)
        x_send(arr, q, True)
        eo[arr, me_dp, pl.ds(q * 16, 16)] = xback[arr, q, me_dp]

    def weight_grad(kind, piece):
        def body(i, carry):
            tile = pl.ds(pl.multiple_of(i * 128, 128), 128)
            total = jnp.zeros((128, 512 if kind < 2 else width), F32)
            for q in (0, 1):
                if kind < 2:
                    lhs = tokin[0, q, pl.ds(0, 8), :, tile].reshape(512, 128)
                    rhs = acts[1 + kind, pl.ds(2 * q, 2)].reshape(512, 512)
                else:
                    lhs = acts[0, pl.ds(2 * q, 2), :, :, tile].reshape(512, 128)
                    rhs = tokin[1, q, pl.ds(0, 8)].reshape(512, width)
                total = total + lax.dot_general(lhs, rhs, TN, preferred_element_type=F32)
            (ggrad, ugrad, dgrad)[kind][tile, :] = total.astype(BF)
            return carry

        tiles = width // 128 if kind < 2 else 4
        lax.fori_loop(piece * tiles // 3, (piece + 1) * tiles // 3, body, 0)
        if piece == 2:
            stores[1 + kind].start()

    def token_side():
        x_wait(0, 0, True)
        x_wait(0, 1, True)
        stores[0].start()
        big = table.astype(BF).astype(F32)
        rest = table - big
        mid = rest.astype(BF).astype(F32)
        small = (rest - mid).astype(BF).astype(F32)
        split_ref[...] = jnp.where(row < 32, big, jnp.where(row < 64, mid, jnp.where(row < 96, small, 0.0))).T.astype(BF)

        def body(share, scores):
            columns = pl.ds(pl.multiple_of(share * width, 128), width)
            outs = eo[0, share]
            return scores + lax.dot_general(outs, ograd[:, columns], NT, preferred_element_type=F32)

        scores = lax.fori_loop(0, 8, body, jnp.zeros((32, 128), F32))
        weighted = chosen[:32] * scores
        for k in range(8):
            hit = (ids[k : k + 1, :] == hosted[:32]).astype(F32)
            pgrad_ref[k : k + 1, :] = jnp.sum(hit * weighted, axis=0, keepdims=True)

    def sent_mid(g, q):
        c_copy(g, q).wait_send()
        wait_out(rs.at[kinds[g], q, pl.ds(0, 3)], rx_s.at[g, q])
        wait_out(acts.at[held[g], q, pl.ds(0, 7)], ag_s.at[g, q])

    def sent_in(arr, q):
        wait_out(xsend.at[arr, q, pl.ds(0, 7)], xs_s.at[arr, q])
        wait_out(ysend.at[arr, q, pl.ds(0, 3)], ys_s.at[arr, q])
        z_sent(arr, q)

    def sent_out(arr, q):
        zb_sent(arr, q)
        wait_out(zout.at[arr, q, :, pl.ds(0, 48)], yb_s.at[arr, q])
        wait_out(xback.at[arr, q, pl.ds(0, 7)], xb_s.at[arr, q])

    T, G = 0, 1
    loads[0].wait()
    gather_rows(T)
    pl.semaphore_wait(barrier, len(partners))
    x_send(T, 0, False)
    x_send(T, 1, False)
    y_stage(T, 0)
    loads[1].wait()
    gather_rows(G)
    x_send(G, 1, False)
    y_stage(T, 1)
    z_far(T, 0)
    z_near(T, 0)
    x_send(G, 0, False)
    z_step(T, 0, 1, R)
    z_step(T, 0, 1, L)
    z_far(T, 1)
    z_near(T, 1)
    z_step(T, 0, 2, R)
    y_stage(G, 0)
    z_step(T, 0, 2, L)
    for load in loads[2:]:
        load.wait()
    forward(T, 0, 0)
    z_step(T, 1, 1, R)
    z_step(T, 1, 1, L)
    z_far(G, 0)
    rs_one(T, 0)
    z_step(T, 0, 3, R)
    z_step(T, 0, 3, L)
    y_stage(G, 1)
    z_step(T, 1, 2, L)
    z_step(T, 1, 2, R)
    rs_two(T, 0)
    forward(T, 1, 0)
    z_step(T, 0, 4, L)
    z_step(T, 0, 4, R)
    z_step(T, 0, 5, R)
    z_near(G, 0)
    z_far(G, 1)
    rs_one(T, 2)
    z_step(T, 1, 3, R)
    z_step(T, 0, 5, L)
    z_step(T, 1, 3, L)
    z_near(G, 1)
    forward(T, 0, 1)
    rs_end(T, 0)
    z_step(G, 0, 1, L)
    rs_one(T, 1)
    z_step(G, 0, 1, R)
    ag_two(T, 0)
    rs_two(T, 1)
    z_step(T, 1, 4, L)
    z_step(T, 1, 4, R)
    z_step(G, 1, 1, L)
    z_step(G, 1, 1, R)
    rs_two(T, 2)
    rs_end(T, 1)
    z_step(G, 0, 2, R)
    z_step(G, 0, 2, L)
    ag_fwd(T, 0)
    forward(G, 0, 0)
    z_step(T, 1, 5, L)
    z_step(T, 1, 5, R)
    forward(T, 1, 1)
    ag_two(T, 1)
    partial_out(T, 0, 0)
    rs_end(T, 2)
    z_step(G, 1, 2, R)
    rs_one(G, 0)
    z_step(G, 1, 2, L)
    ag_fwd(T, 1)
    rs_one(T, 3)
    z_step(G, 0, 3, R)
    partial_out(T, 0, 1)
    zb_begin(T, 0)
    z_step(G, 0, 3, L)
    forward(G, 1, 0)
    rs_two(T, 3)
    rs_two(G, 0)
    ag_two(T, 2)
    z_step(G, 0, 4, L)
    z_step(G, 0, 4, R)
    rs_one(G, 2)
    z_step(G, 1, 3, R)
    z_step(G, 1, 3, L)
    rs_end(T, 3)
    rs_end(G, 0)
    z_step(G, 0, 5, L)
    ag_fwd(T, 2)
    z_step(G, 0, 5, R)
    forward(G, 0, 1)
    ag_two(T, 3)
    rs_two(G, 2)
    rs_one(G, 1)
    partial_out(T, 1, 0)
    ag_fwd(T, 3)
    z_step(G, 1, 4, L)
    z_step(G, 1, 4, R)
    rs_two(G, 1)
    partial_out(T, 1, 1)
    zb_begin(T, 1)
    zb_step(T, 0, 4, R)
    ag_two(G, 0)
    rs_end(G, 1)
    zb_step(T, 0, 4, L)
    ag_fwd(G, 0)
    z_step(G, 1, 5, L)
    z_step(G, 1, 5, R)
    rs_end(G, 2)
    forward(G, 1, 1)
    ag_two(G, 1)
    zb_step(T, 1, 4, R)
    weight_grad(2, 0)
    rs_one(G, 3)
    zb_step(T, 1, 4, L)
    zb_step(T, 0, 3, R)
    ag_fwd(G, 1)
    rs_two(G, 3)
    partial_out(G, 0, 0)
    partial_out(G, 0, 1)
    zb_begin(G, 0)
    zb_step(T, 1, 3, L)
    zb_step(T, 1, 3, R)
    rs_end(G, 3)
    ag_two(G, 2)
    zb_step(T, 0, 3, L)
    ag_two(G, 3)
    zb_step(G, 0, 4, R)
    zb_step(T, 0, 2, R)
    zb_step(T, 0, 2, L)
    ag_fwd(G, 2)
    zb_step(G, 0, 4, L)
    weight_grad(2, 1)
    zb_step(T, 1, 2, R)
    ag_fwd(G, 3)
    partial_out(G, 1, 0)
    zb_step(T, 1, 2, L)
    partial_out(G, 1, 1)
    zb_begin(G, 1)
    zb_step(G, 0, 3, L)
    zb_step(G, 0, 3, R)
    zb_step(T, 0, 1, L)
    zb_step(G, 1, 4, L)
    zb_step(T, 0, 1, R)
    zb_step(G, 1, 4, R)
    zb_step(G, 0, 2, R)
    zb_step(T, 1, 1, L)
    weight_grad(0, 0)
    weight_grad(1, 0)
    zb_step(G, 1, 3, R)
    zb_step(T, 1, 1, R)
    zb_step(G, 1, 3, L)
    weight_grad(2, 2)
    weight_grad(0, 1)
    zb_step(G, 0, 2, L)
    weight_grad(1, 1)
    zb_step(G, 1, 2, R)
    zb_step(G, 0, 1, R)
    zb_step(G, 1, 2, L)
    zb_end(T, 0)
    zb_step(G, 0, 1, L)
    zb_end(T, 1)
    zb_step(G, 1, 1, R)
    zb_step(G, 1, 1, L)
    x_back(T, 0)
    zb_end(G, 0)
    x_back(T, 1)
    zb_end(G, 1)
    weight_grad(0, 2)
    x_back(G, 0)
    weight_grad(1, 2)
    x_back(G, 1)
    token_side()
    for arr in (T, G):
        for q in (0, 1):
            sent_in(arr, q)
        for m in range(4):
            sent_mid(arr, m)
    for arr, q in ((T, 0), (T, 1), (G, 0)):
        sent_out(arr, q)
    x_wait(G, 0, True)
    x_wait(G, 1, True)
    stores[4].start()
    sent_out(G, 1)
    for store in stores:
        store.wait()


def finish(width, eo_in, ggrad_in, ugrad_in, dgrad_in, split, select, pgrad_in, mixed, igrad, pgrad, ggrad, ugrad, dgrad, eo, gbuf, ubuf, dbuf, mtile, itile, esem, isem, osem, tsem):
    rows = [pltpu.make_async_copy(eo_in.at[a, pl.ds(4 * h, 4)], eo.at[a, pl.ds(4 * h, 4)], esem.at[a, h]) for h in (0, 1) for a in (0, 1)]
    moves = ((ggrad_in, gbuf, ggrad), (ugrad_in, ubuf, ugrad), (dgrad_in, dbuf, dgrad))
    come = [pltpu.make_async_copy(a, b, isem.at[i]) for i, (a, b, _) in enumerate(moves)]
    leave = [pltpu.make_async_copy(b, o, osem.at[i]) for i, (_, b, o) in enumerate(moves)]
    for move in rows + come:
        move.start()
    pgrad[...] = pgrad_in[...]
    outs = []
    for pair in range(4):
        if pair % 2 == 0:
            rows[pair].wait()
            rows[pair + 1].wait()
        else:
            for k in ((0,), (1, 2))[pair // 2]:
                come[k].wait()
                leave[k].start()
        for share in (2 * pair, 2 * pair + 1):
            columns = pl.ds(share * width, width)
            mtile[:, columns] = jnp.dot(split[...], jnp.concatenate([eo[0, share]] * 4, axis=0), preferred_element_type=F32).astype(BF)
            itile[:, columns] = lax.dot_general(select[...], eo[1, share], TN, preferred_element_type=F32).astype(BF)
        columns = pl.ds(2 * pair * width, 2 * width)
        for k, (tile, to) in enumerate(((mtile, mixed), (itile, igrad))):
            outs.append(pltpu.make_async_copy(tile.at[:, columns], to.at[:, columns], tsem.at[k, pair]))
            outs[-1].start()
    for out in outs + leave:
        out.wait()


def on_device(tokens, out_grad, expert_ids, route_probs, hosted, gate_weight, up_weight, down_weight):
    model_width = tokens.shape[1]
    width, hidden = gate_weight.shape
    vmem = pl.BlockSpec(memory_space=pltpu.VMEM)
    smem = pl.BlockSpec(memory_space=pltpu.SMEM)
    hbm = pl.BlockSpec(memory_space=pl.ANY)
    dma = pltpu.SemaphoreType.DMA
    row_shape = jax.ShapeDtypeStruct(tokens.shape, BF)
    side_shape = jax.ShapeDtypeStruct((8, 128), F32)
    grads = (
        jax.ShapeDtypeStruct(gate_weight.shape, BF),
        jax.ShapeDtypeStruct(up_weight.shape, BF),
        jax.ShapeDtypeStruct(down_weight.shape, BF),
    )
    split, pgrad, ggrad, ugrad, dgrad, eo, select = pl.pallas_call(
        functools.partial(kernel, width),
        out_shape=(
            jax.ShapeDtypeStruct((128, 128), BF), side_shape, *grads,
            jax.ShapeDtypeStruct((2, 8, 32, width), BF),
            jax.ShapeDtypeStruct((32, 128), BF),
        ),
        in_specs=[vmem, vmem, smem] + [hbm] * 5,
        out_specs=(vmem, vmem, hbm, hbm, hbm, hbm, vmem),
        scratch_shapes=[
            pltpu.VMEM((128, model_width), BF),
            pltpu.VMEM((128, model_width), BF),
            pltpu.VMEM((width, hidden), BF),
            pltpu.VMEM((width, hidden), BF),
            pltpu.VMEM((hidden, width), BF),
            pltpu.VMEM((width, hidden), BF),
            pltpu.VMEM((width, hidden), BF),
            pltpu.VMEM((hidden, width), BF),
            pltpu.VMEM((2, 2, 8, 16, width), BF),
            pltpu.VMEM((2, 2, 8, 16, width), BF),
            pltpu.VMEM((2, 2, 4, 2, 16, width), BF),
            pltpu.VMEM((2, 2, 2, 64, width), BF),
            pltpu.VMEM((2, 2, 10, 64, width), BF),
            pltpu.VMEM((3, 4, 4, 2, 32, hidden), F32),
            pltpu.VMEM((3, 4, 4, 32, hidden), F32),
            pltpu.VMEM((2, 3, 4, 32, hidden // 2), F32),
            pltpu.VMEM((4, 3, 4, 32, hidden // 2), F32),
            pltpu.VMEM((3, 4, 32, hidden), F32),
            pltpu.VMEM((3, 4, 8, 32, hidden), BF),
            pltpu.VMEM((2, 2, 8, 64, width), BF),
            pltpu.VMEM((2, 2, 2, 2, 5, 64, width), BF),
            pltpu.VMEM((2, 2, 2, 64, width), BF),
            pltpu.VMEM((2, 2, 4, 2, 16, width), BF),
            pltpu.VMEM((2, 2, 8, 16, width), BF),
            pltpu.VMEM((2, 8, 32, width), BF),
            pltpu.VMEM((128, 128), BF),
            pltpu.VMEM((128, 128), BF),
            dma((5,)), dma((5,)),
            dma((2, 2)), dma((2, 2)), dma((2, 2)), dma((2, 2)),
            dma((2, 2, 2, 2)), dma((2, 2, 2, 6, 2)),
            dma((2, 4)), dma((2, 4)), dma((2, 4)), dma((2, 4, 3)), dma((2, 4)), dma((2, 4, 4)),
            dma((2, 2, 2, 2)), dma((2, 2, 2, 6, 2)), dma((2, 2)), dma((2, 2)), dma((2, 2)), dma((2, 2)),
        ],
        compiler_params=pltpu.CompilerParams(
            collective_id=0, has_side_effects=True, vmem_limit_bytes=60 * 1024 * 1024
        ),
        cost_estimate=pl.CostEstimate(flops=9 * 2 * 1024 * 896 * 512, bytes_accessed=16_000_000, transcendentals=65536),
    )(expert_ids.T, route_probs.T, hosted, tokens, out_grad, gate_weight, up_weight, down_weight)
    mixed, igrad, pgrad, ggrad, ugrad, dgrad = pl.pallas_call(
        functools.partial(finish, width),
        out_shape=(row_shape, row_shape, side_shape, *grads),
        in_specs=[hbm] * 4 + [vmem] * 3,
        out_specs=(hbm, hbm, vmem, hbm, hbm, hbm),
        scratch_shapes=[
            pltpu.VMEM((2, 8, 32, width), BF),
            pltpu.VMEM((width, hidden), BF),
            pltpu.VMEM((width, hidden), BF),
            pltpu.VMEM((hidden, width), BF),
            pltpu.VMEM((128, model_width), BF),
            pltpu.VMEM((128, model_width), BF),
            dma((2, 2)), dma((3,)), dma((3,)), dma((2, 4)),
        ],
        compiler_params=pltpu.CompilerParams(vmem_limit_bytes=60 * 1024 * 1024),
    )(eo, ggrad, ugrad, dgrad, split, select, pgrad)
    return mixed, igrad, pgrad.T, ggrad, ugrad, dgrad


def solution(mesh):
    return jax.shard_map(
        on_device,
        mesh=mesh,
        in_specs=(
            P(("dp", "expert"), None),
            P(("dp", "expert"), None),
            P(("dp", "expert"), None),
            P(("dp", "expert"), None),
            P(),
            P("dp", "expert"),
            P("dp", "expert"),
            P("expert", "dp"),
        ),
        out_specs=(
            P(("dp", "expert"), None),
            P(("dp", "expert"), None),
            P(("dp", "expert"), None),
            P("dp", "expert"),
            P("dp", "expert"),
            P("expert", "dp"),
        ),
        check_vma=False,
    )
```
